32 devices in a mesh: groups: 2 (over y), row: 4 (over z), col: 4 (over x, core).
Axes of the slice: x: 2, y: 2, z: 4, core: 2. Of those that a mesh axis runs over, the one named last changes fastest.
Arguments:
- features: bfloat16 [4096, 256], P(('groups', 'row', 'col')), parts along dimension 0, may hold values from -6 to 6
- w_self: bfloat16 [256, 256], replicated, may hold values from -0.375 to 0.375
- w_neigh: bfloat16 [256, 256], replicated, may hold values from -0.375 to 0.375
- layer_bias: float32 [256], replicated, may hold values from -4 to 4
- tile_vals: bfloat16 [8, 4, 8, 128, 128], P(('groups', 'row'), 'col'), parts along dimension 0, may hold values from 0 to 2
- tile_dst: int32 [8, 4, 8], P(('groups', 'row'), 'col'), parts along dimension 0, may hold values from 0 to 3, as said below
- tile_src: int32 [8, 4, 8], P(('groups', 'row'), 'col'), parts along dimension 0, may hold values from 0 to 3
- tile_count: int32 [8, 4], P(('groups', 'row'), 'col'), parts along dimension 0, may hold values from 2 to 8, as said below
- degree: int32 [4096], P(('groups', 'row', 'col')), parts along dimension 0, may hold values from 8 to 32
- target_ids: int32 [512], P('groups'), parts along dimension 0, may hold values from 0 to 2047, as said below
- cotangent: bfloat16 [4096, 256], P(('groups', 'row', 'col')), parts along dimension 0, may hold values from -6 to 6
Outputs:
- hidden: bfloat16 [4096, 256], P(('groups', 'row', 'col')), parts along dimension 0
- grad_features: bfloat16 [4096, 256], P(('groups', 'row', 'col')), parts along dimension 0
- grad_self: float32 [512, 256], P('groups'), parts along dimension 0
- grad_neigh: float32 [512, 256], P('groups'), parts along dimension 0
- grad_bias: float32 [512], P('groups'), parts along dimension 0
The draws below stay inside these ranges and needn't reach their ends.
There are 2 independent parts, one for each index of `groups`. The reference program is written for one: setup_inputs(seed, part) draws one part's arguments, and reference() takes and returns one part's arrays. A program takes and returns all parts, laid end to end along the dimension named above; an argument that names none is the same for every part. Nothing has to cross between parts.
Inputs may be any that keep to these rules, and one draw needn't show every extreme that they name: Within one grid cell the 8 pairs (tile_dst, tile_src) are all different. Slots at or beyond tile_count of their cell are not part of the graph; some cell uses all 8 slots. `target_ids`: distinct node numbers.
All inputs are finite; a program needn't handle non-finite values.
Results may differ from the reference program's by a relative error of at most 0.0055.
Values may be sent and summed in bfloat16 or wider, within the bound.
No kernel may reach another device: no remote copies, remote signals or barrier semaphores. Data moves between devices by JAX's collectives and lax.ppermute only.
A program may use at most 64 MiB of HBM per device.

```python
import math
import jax
import jax.numpy as jnp
from jax import lax

F = 256
H = 256
TL = 128
ND = 128
KT = 8
NODES = 2048
TARGETS = 256
N_ROW = 4
N_COL = 4


def tile_pairs(key):
    n_dst = N_COL * ND // TL
    n_src = N_ROW * ND // TL
    keys = jax.random.split(key, N_ROW * N_COL)
    picks = jax.vmap(lambda single: jax.random.permutation(single, n_dst * n_src)[:KT])(keys)
    return (picks.reshape(N_ROW, N_COL, KT).astype(jnp.int32), n_src)


def draw_tile_dst(key, part):
    picks, n_src = tile_pairs(key)
    return (picks // n_src).astype(jnp.int32)


def draw_tile_src(key, part):
    picks, n_src = tile_pairs(key)
    return (picks % n_src).astype(jnp.int32)


def draw_tile_count(key, part):
    key = jax.random.fold_in(key, 5)
    first_key, second_key = jax.random.split(key)
    counts = jax.random.randint(first_key, (N_ROW * N_COL,), KT // 4, KT + 1)
    fullest = jax.random.randint(second_key, (), 0, N_ROW * N_COL)
    counts = jnp.where(jnp.arange(N_ROW * N_COL) == fullest, KT, counts)
    return counts.reshape(N_ROW, N_COL).astype(jnp.int32)


def draw_tile_vals(key, part):
    key = jax.random.fold_in(key, 11)
    first_key, second_key = jax.random.split(key)
    shape = (N_ROW, N_COL, KT, TL, TL)
    kept = jax.random.bernoulli(first_key, 0.05, shape)
    weights = jax.random.uniform(second_key, shape, jnp.float32, 0.5, 1.5)
    return jnp.where(kept, weights, 0.0).astype(jnp.float32).astype(jnp.bfloat16)


def draw_target_ids(key, part):
    key = jax.random.fold_in(key, 7)
    first_key, second_key = jax.random.split(key)
    inner = (jax.random.permutation(first_key, NODES - 2)[:TARGETS - 2] + 1).astype(jnp.int32)
    ends = jnp.array([0, NODES - 1], jnp.int32)
    return jax.random.permutation(second_key, jnp.concatenate([inner, ends])).astype(jnp.int32)


def with_ends(entries, rng, least, high):
    spot = [jax.random.randint(jax.random.fold_in(rng, axis), (), 0, length) for axis, length in enumerate(entries.shape)]
    longest = entries.shape.index(max(entries.shape))
    next_to = spot[:longest] + [(spot[longest] + 1) % entries.shape[longest]] + spot[longest + 1:]
    return entries.at[tuple(spot)].set(least).at[tuple(next_to)].set(high)


def level_of(own_key, dims, cuts, smallest, top_value):
    def one(axis_at, shards_of):
        steps = jax.random.uniform(jax.random.fold_in(jax.random.fold_in(own_key, 6), axis_at), (shards_of,), jnp.float32, smallest / len(cuts), top_value / len(cuts))
        return jnp.repeat(jnp.exp(steps), dims[axis_at] // shards_of).reshape((-1,) + (1,) * (len(dims) - axis_at - 1))

    factor_of = one(*cuts[0])
    for cut in cuts[1:]:
        factor_of = factor_of * one(*cut)
    return factor_of


def bell_draw(rng, shape, width, bound, cuts=(), kind=jnp.bfloat16):
    factor_of = level_of(rng, shape, cuts, -0.22, 0.18) if cuts else 1.0
    values = jax.random.normal(rng, shape, jnp.float32) * width * factor_of
    return jnp.minimum(jnp.maximum(values, -bound), bound).astype(kind)


def setup_inputs(seed: int = 0, part: int = 0) -> dict:
    key_list = jax.random.split(jax.random.key(seed), 12)
    part_splits = jax.random.split(jax.random.fold_in(key_list[11], part), 12)
    return {
        "features": bell_draw(part_splits[0], (NODES, F), 1.0, 6.0, ((0, 16),)),
        "w_self": bell_draw(key_list[1], (F, H), F ** -0.5, 0.375),
        "w_neigh": bell_draw(key_list[2], (F, H), F ** -0.5, 0.375),
        "layer_bias": bell_draw(key_list[3], (H,), 1.0, 4.0, (), jnp.float32),
        "tile_vals": draw_tile_vals(jax.random.fold_in(jax.random.fold_in(key_list[11], part), 71), part),
        "tile_dst": draw_tile_dst(jax.random.fold_in(jax.random.fold_in(key_list[11], part), 71), part),
        "tile_src": draw_tile_src(jax.random.fold_in(jax.random.fold_in(key_list[11], part), 71), part),
        "tile_count": draw_tile_count(jax.random.fold_in(jax.random.fold_in(key_list[11], part), 71), part),
        "degree": with_ends(jax.random.randint(part_splits[8], (NODES,), 8, 33), jax.random.fold_in(part_splits[8], 1), 8, 32).astype(jnp.int32),
        "target_ids": draw_target_ids(jax.random.fold_in(jax.random.fold_in(key_list[11], part), 71), part),
        "cotangent": bell_draw(part_splits[10], (NODES, H), 1.0, 6.0, ((0, 16),)),
    }


HIGHEST = lax.Precision.HIGHEST

def gelu_value(inputs):
    return 0.5 * inputs * (1.0 + jax.scipy.special.erf(inputs * 0.7071067811865476))

def gelu_slope(inputs):
    return 0.5 * (1.0 + jax.scipy.special.erf(inputs * 0.7071067811865476)) + inputs * jnp.exp(-0.5 * inputs * inputs) * 0.3989422804014327

def tile_sum(values, take_index, put_index, usable, source, out_tiles, transpose):
    slot_count, tile_width = (values.shape[0], values.shape[1])
    columns = source.shape[1]
    blocks = source.reshape(-1, tile_width, columns)
    group_size = math.gcd(slot_count, 16)
    pattern = 'kji,kjf->kif' if transpose else 'kij,kjf->kif'

    def advance(running, offset):
        tile_block = lax.dynamic_slice_in_dim(values, offset, group_size, 0).astype(jnp.float32)
        taken = lax.dynamic_slice_in_dim(take_index, offset, group_size, 0)
        placed = lax.dynamic_slice_in_dim(put_index, offset, group_size, 0)
        allowed = lax.dynamic_slice_in_dim(usable, offset, group_size, 0)
        chosen = blocks[taken].astype(jnp.float32)
        product = jnp.einsum(pattern, tile_block, chosen, precision=HIGHEST)
        product = product * allowed.astype(jnp.float32)[:, None, None]
        running = running.at[placed].add(product)
        return (running, None)
    offsets = jnp.arange(0, slot_count, group_size, dtype=jnp.int32)
    running, _ = lax.scan(advance, jnp.zeros((out_tiles, tile_width, columns), jnp.float32), offsets)
    return running.reshape(out_tiles * tile_width, columns)

def reference(features, w_self, w_neigh, layer_bias, tile_vals, tile_dst, tile_src, tile_count, degree, target_ids, cotangent):
    grid = features.reshape(N_ROW, N_COL, ND, F)
    dst_tiles = N_COL * ND // TL
    src_tiles = N_ROW * ND // TL
    slot_index = jnp.arange(KT, dtype=jnp.int32)
    places = jnp.arange(N_ROW * N_COL, dtype=jnp.int32)

    def forward_cell(running, place):
        grid_row = place // N_COL
        grid_col = place % N_COL
        source = lax.dynamic_index_in_dim(grid, grid_col, 1, keepdims=False).reshape(N_ROW * ND, F)
        usable = slot_index < tile_count[grid_row, grid_col]
        cell_part = tile_sum(tile_vals[grid_row, grid_col], tile_src[grid_row, grid_col], tile_dst[grid_row, grid_col], usable, source, dst_tiles, False)
        return (running.at[grid_row].add(cell_part), None)
    agg_sum, _ = lax.scan(forward_cell, jnp.zeros((N_ROW, N_COL * ND, F), jnp.float32), places)
    inv_degree = 1.0 / degree.astype(jnp.float32)
    aggregate = (agg_sum.reshape(NODES, F) * inv_degree[:, None]).astype(jnp.bfloat16)
    before = jnp.dot(features, w_self, preferred_element_type=jnp.float32) + jnp.dot(aggregate, w_neigh, preferred_element_type=jnp.float32) + layer_bias
    hidden = gelu_value(before).astype(jnp.bfloat16)
    target = jnp.zeros((NODES,), jnp.float32).at[target_ids].set(1.0)
    slope_grad = (cotangent.astype(jnp.float32) * target[:, None] * gelu_slope(before)).astype(jnp.bfloat16)
    grad_scale = 1.0 / math.sqrt(NODES)
    grad_self = jnp.dot(features.T, slope_grad, preferred_element_type=jnp.float32) * grad_scale
    grad_neigh = jnp.dot(aggregate.T, slope_grad, preferred_element_type=jnp.float32) * grad_scale
    grad_bias = lax.optimization_barrier(jnp.sum(slope_grad.astype(jnp.float32), axis=0)) * grad_scale
    message = (lax.dot_general(slope_grad, w_neigh, (((1,), (1,)), ((), ())), preferred_element_type=jnp.float32) * inv_degree[:, None]).astype(jnp.bfloat16)
    message_grid = message.reshape(N_ROW, N_COL * ND, F)

    def backward_cell(running, place):
        grid_row = place // N_COL
        grid_col = place % N_COL
        usable = slot_index < tile_count[grid_row, grid_col]
        cell_part = tile_sum(tile_vals[grid_row, grid_col], tile_dst[grid_row, grid_col], tile_src[grid_row, grid_col], usable, message_grid[grid_row], src_tiles, True)
        rounded = lax.optimization_barrier(cell_part.astype(jnp.bfloat16)).astype(jnp.float32)
        return (running.at[grid_col].add(rounded), None)
    back_sum, _ = lax.scan(backward_cell, jnp.zeros((N_COL, N_ROW * ND, F), jnp.float32), places)
    neighbour_grad = back_sum.reshape(N_COL, N_ROW, ND, F).transpose(1, 0, 2, 3).reshape(NODES, F)
    direct = lax.dot_general(slope_grad, w_self, (((1,), (1,)), ((), ())), preferred_element_type=jnp.float32)
    grad_features = (direct + neighbour_grad).astype(jnp.bfloat16)
    return (hidden, grad_features, grad_self, grad_neigh, grad_bias)
```

```python
import math

import jax
import jax.numpy as jnp
from jax import lax
from jax.sharding import PartitionSpec as P

F32 = jnp.float32
BF16 = jnp.bfloat16


def gelu_value(inputs):
    return 0.5 * inputs * (1.0 + jax.scipy.special.erf(inputs * 0.7071067811865476))


def gelu_slope(inputs):
    return (
        0.5 * (1.0 + jax.scipy.special.erf(inputs * 0.7071067811865476))
        + inputs * jnp.exp(-0.5 * inputs * inputs) * 0.3989422804014327
    )


def dot(left, right, dims=((1,), (0,))):
    return lax.dot_general(left, right, (dims, ((), ())), preferred_element_type=F32)


def shift(block, axis, step):
    size = lax.axis_size(axis)
    return lax.ppermute(block, axis, [(i, (i + step) % size) for i in range(size)])


def gather_parts(block, axis):
    size = lax.axis_size(axis)
    return [block] + [shift(block, axis, -step) for step in range(1, size)]


def swap_parts(parts, axis):
    return [parts[0]] + [shift(parts[j], axis, j) for j in range(1, len(parts))]


def compact_device(
    features,
    w_self,
    w_neigh,
    layer_bias,
    tile_vals,
    tile_dst,
    tile_src,
    tile_count,
    degree,
    target_ids,
    cotangent,
):
    rows = lax.axis_size("row")
    cols = lax.axis_size("col")
    row = lax.axis_index("row")
    col = lax.axis_index("col")
    nodes, width = features.shape
    slots = target_ids.shape[0]
    share = slots // cols
    tiles = tile_vals[0, 0]

    feature_parts = gather_parts(features, "row")

    ids = lax.dynamic_slice_in_dim(jnp.concatenate([target_ids, target_ids]), col * share, slots, 0)
    place = jnp.arange(cols * nodes, dtype=jnp.int32)
    slab = (row * cols + (col + place // nodes) % cols) * nodes + place % nodes
    pick_slab = (ids[:, None] == slab[None, :]).astype(BF16)
    pick_own = pick_slab[:, :nodes]

    degree_wide = jnp.broadcast_to(degree.astype(BF16)[:, None], (nodes, 128))
    known = dot(pick_own, jnp.concatenate([features, cotangent, degree_wide], axis=1)).astype(BF16)
    known = sum(swap_parts([known[j * share : (j + 1) * share] for j in range(cols)], "col"))
    feature_slots = known[:, :width]
    cotangent_slots = known[:, width : 2 * width]
    degree_slots = known[:, 2 * width :]

    usable = jnp.arange(tiles.shape[0], dtype=jnp.int32) < tile_count[0, 0]
    src = (tile_src[0, 0] - row) % rows
    dst = (tile_dst[0, 0] - col) % cols
    src = jnp.where(usable, src, rows)
    adjacency = jnp.zeros((rows, cols, nodes, nodes), BF16).at[src, dst].set(tiles, mode="drop")
    adjacency = adjacency.reshape(rows, cols * nodes, nodes)
    picked = [dot(pick_slab, adjacency[s]).astype(BF16) for s in range(rows)]
    own_columns = sum(swap_parts(picked, "row"))

    slab_features = jnp.concatenate(feature_parts, axis=0)
    part = dot(jnp.concatenate(picked, axis=1), slab_features)
    part_low = part.astype(BF16)
    agg_parts = swap_parts(
        [part[:share]] + [part_low[j * share : (j + 1) * share] for j in range(1, cols)], "col"
    )
    agg_sum = sum(piece.astype(F32) for piece in agg_parts)
    degree_one = degree_slots[:, :1].astype(F32)
    inverse = jnp.where(degree_one > 0, 1.0 / jnp.maximum(degree_one, 1.0), 0.0)
    aggregate = (agg_sum * inverse).astype(BF16)
    before = dot(feature_slots, w_self) + dot(aggregate, w_neigh) + layer_bias
    slope = (cotangent_slots.astype(F32) * gelu_slope(before)).astype(BF16)

    fixed = jnp.concatenate([feature_slots, degree_slots], axis=1)
    fixed = sum(gather_parts(fixed, "row"))
    found = jnp.concatenate([slope, aggregate], axis=1)
    found = sum(gather_parts(found, "row"))
    everything = jnp.concatenate(
        gather_parts(jnp.concatenate([found, fixed], axis=1), "col"), axis=0
    )
    slope_all = everything[:, :width]
    terms = dot(everything[:, width : 3 * width], slope_all, ((0,), (0,)))
    scale = 1.0 / math.sqrt(nodes * rows * cols)
    grad_neigh = terms[:width] * scale
    grad_self = terms[width:] * scale
    grad_bias = jnp.sum(slope_all.astype(F32), axis=0) * scale
    degree_all = everything[:, 3 * width : 3 * width + 1].astype(F32)
    message = (dot(slope_all, w_neigh, ((1,), (1,))) / degree_all).astype(BF16)
    own_slope = dot(pick_own, slope_all, ((0,), (0,))).astype(BF16)
    grad_features = dot(own_slope, w_self, ((1,), (1,))) + dot(own_columns, message, ((0,), (0,)))

    dense = sum(dot(adjacency[s], feature_parts[s]) for s in range(rows))
    dense_low = dense.astype(BF16)
    dense_parts = swap_parts(
        [dense[:nodes]] + [dense_low[j * nodes : (j + 1) * nodes] for j in range(1, cols)], "col"
    )
    own_sum = sum(piece.astype(F32) for piece in dense_parts)
    own_aggregate = (own_sum * (1.0 / degree.astype(F32))[:, None]).astype(BF16)
    own_before = dot(features, w_self) + dot(own_aggregate, w_neigh) + layer_bias
    hidden = gelu_value(own_before).astype(BF16)
    return (hidden, grad_features.astype(BF16), grad_self, grad_neigh, grad_bias)


def tile_sum(values, take_index, put_index, usable, source, out_tiles, transpose, first_tile):
    slot_count, tile_width = (values.shape[0], values.shape[1])
    columns = source.shape[1]
    blocks = source.reshape(-1, tile_width, columns)
    group_size = math.gcd(slot_count, 16)
    pattern = "kji,kjf->kif" if transpose else "kij,kjf->kif"

    def advance(running, offset):
        tile_block = lax.dynamic_slice_in_dim(values, offset, group_size, 0)
        taken = lax.dynamic_slice_in_dim(take_index, offset, group_size, 0)
        placed = lax.dynamic_slice_in_dim(put_index, offset, group_size, 0) - first_tile
        allowed = lax.dynamic_slice_in_dim(usable, offset, group_size, 0)
        inside = allowed & (placed >= 0) & (placed < out_tiles)
        chosen = blocks[taken]
        product = jnp.einsum(pattern, tile_block, chosen, preferred_element_type=jnp.float32)
        product = product * inside.astype(jnp.float32)[:, None, None]
        where_to = jnp.where(inside, placed, 0)
        running = running.at[where_to].add(product)
        return (running, None)

    offsets = jnp.arange(0, slot_count, group_size, dtype=jnp.int32)
    running, _ = lax.scan(
        advance, jnp.zeros((out_tiles, tile_width, columns), jnp.float32), offsets
    )
    return running.reshape(out_tiles * tile_width, columns)


def dense_device(
    features,
    w_self,
    w_neigh,
    layer_bias,
    tile_vals,
    tile_dst,
    tile_src,
    tile_count,
    degree,
    target_ids,
    cotangent,
):
    row_count = lax.axis_size("row")
    col_count = lax.axis_size("col")
    node_rows = features.shape[0]
    tile_width = tile_vals.shape[-1]
    cell_tiles = tile_vals[0, 0]
    cell_dst = tile_dst[0, 0]
    cell_src = tile_src[0, 0]
    usable = jnp.arange(cell_tiles.shape[0], dtype=jnp.int32) < tile_count[0, 0]
    source = lax.all_gather(features, "row", axis=0, tiled=True)
    partial_value = tile_sum(
        cell_tiles,
        cell_src,
        cell_dst,
        usable,
        source,
        col_count * node_rows // tile_width,
        False,
        0,
    )
    agg_sum = lax.psum_scatter(partial_value, "col", scatter_dimension=0, tiled=True)
    inv_degree = 1.0 / degree.astype(jnp.float32)
    aggregate = (agg_sum * inv_degree[:, None]).astype(jnp.bfloat16)
    before = (
        jnp.dot(features, w_self, preferred_element_type=jnp.float32)
        + jnp.dot(aggregate, w_neigh, preferred_element_type=jnp.float32)
        + layer_bias
    )
    hidden = gelu_value(before).astype(jnp.bfloat16)
    first_node = (lax.axis_index("row") * col_count + lax.axis_index("col")) * node_rows
    node_ids = first_node + jnp.arange(node_rows, dtype=jnp.int32)
    target = jnp.any(node_ids[:, None] == target_ids[None, :], axis=1).astype(jnp.float32)
    slope_grad = (cotangent.astype(jnp.float32) * target[:, None] * gelu_slope(before)).astype(
        jnp.bfloat16
    )
    grad_scale = 1.0 / math.sqrt(node_rows * row_count * col_count)
    contract_rows = (((0,), (0,)), ((), ()))
    self_term = lax.dot_general(
        features, slope_grad, contract_rows, preferred_element_type=jnp.float32
    )
    neigh_term = lax.dot_general(
        aggregate, slope_grad, contract_rows, preferred_element_type=jnp.float32
    )
    bias_term = jnp.sum(slope_grad.astype(jnp.float32), axis=0)
    self_sum, neigh_sum, bias_sum = lax.psum((self_term, neigh_term, bias_term), ("row", "col"))
    contract_out = (((1,), (1,)), ((), ()))
    message = (
        lax.dot_general(slope_grad, w_neigh, contract_out, preferred_element_type=jnp.float32)
        * inv_degree[:, None]
    ).astype(jnp.bfloat16)
    message_slab = lax.all_gather(message, "col", axis=0, tiled=True)
    back_part = tile_sum(
        cell_tiles,
        cell_dst,
        cell_src,
        usable,
        message_slab,
        row_count * node_rows // tile_width,
        True,
        0,
    )
    neighbour_grad = lax.psum_scatter(
        back_part.astype(jnp.bfloat16).astype(jnp.float32).astype(jnp.bfloat16),
        "row",
        scatter_dimension=0,
        tiled=True,
    ).astype(jnp.float32)
    direct = lax.dot_general(slope_grad, w_self, contract_out, preferred_element_type=jnp.float32)
    grad_features = (direct + neighbour_grad).astype(jnp.bfloat16)
    return (
        hidden,
        grad_features,
        self_sum * grad_scale,
        neigh_sum * grad_scale,
        bias_sum * grad_scale,
    )


def solution(mesh):
    in_specs = (
        P(("groups", "row", "col"), None),
        P(),
        P(),
        P(),
        P(("groups", "row"), "col", None, None, None),
        P(("groups", "row"), "col", None),
        P(("groups", "row"), "col", None),
        P(("groups", "row"), "col"),
        P(("groups", "row", "col")),
        P("groups"),
        P(("groups", "row", "col"), None),
    )
    out_specs = (
        P(("groups", "row", "col"), None),
        P(("groups", "row", "col"), None),
        P("groups", None),
        P("groups", None),
        P("groups"),
    )
    parts = mesh.shape["row"] * mesh.shape["col"]
    per_device = compact_device if parts <= 16 else dense_device
    return jax.shard_map(
        per_device, mesh=mesh, in_specs=in_specs, out_specs=out_specs, check_vma=False
    )
```

```python
import math

import jax
import jax.numpy as jnp
from jax import lax
from jax.sharding import PartitionSpec as P

F32 = jnp.float32
BF16 = jnp.bfloat16


def gelu_value(inputs):
    return 0.5 * inputs * (1.0 + jax.scipy.special.erf(inputs * 0.7071067811865476))


def gelu_slope(inputs):
    return (
        0.5 * (1.0 + jax.scipy.special.erf(inputs * 0.7071067811865476))
        + inputs * jnp.exp(-0.5 * inputs * inputs) * 0.3989422804014327
    )


def dot(left, right, dims=((1,), (0,))):
    return lax.dot_general(left, right, (dims, ((), ())), preferred_element_type=F32)


def trade(block, axis, step):
    return lax.ppermute(block, axis, [(i, i ^ step) for i in range(lax.axis_size(axis))])


def flip(pair, axis, bit):
    return jnp.where(bit == 1, jnp.flip(pair, axis), pair)


def compact_device(
    features,
    w_self,
    w_neigh,
    layer_bias,
    tile_vals,
    tile_dst,
    tile_src,
    tile_count,
    degree,
    target_ids,
    cotangent,
):
    rows = lax.axis_size("row")
    cols = lax.axis_size("col")
    row = lax.axis_index("row")
    col = lax.axis_index("col")
    low, high = col % 2, col // 2
    nodes, width = features.shape
    slots = target_ids.shape[0]
    share = slots // cols
    half = slots // 2
    tiles = tile_vals[0, 0]

    feature_parts = [features] + [trade(features, "row", s) for s in range(1, rows)]

    ids = jnp.swapaxes(target_ids.reshape(2, 2, share), 0, 1)
    ids = flip(flip(ids, 0, low), 1, high).reshape(slots)
    place = jnp.arange(cols * nodes, dtype=jnp.int32)
    turn = place // nodes
    slab = (row * cols + (col ^ (turn // 2 + turn % 2 * 2))) * nodes + place % nodes
    pick_slab = (ids[:, None] == slab[None, :]).astype(BF16)
    pick_own = pick_slab[:, :nodes]
    column = ((row ^ turn) * cols + col) * nodes + place % nodes
    pick_column = (ids[:, None] == column[None, :]).astype(BF16)

    usable = jnp.arange(tiles.shape[0], dtype=jnp.int32) < tile_count[0, 0]
    src = tile_src[0, 0] ^ row
    dst = tile_dst[0, 0] ^ col
    src = jnp.where(usable, src, rows)
    dst = dst // 2 + dst % 2 * 2
    adjacency = jnp.zeros((rows, cols, nodes, nodes), BF16).at[src, dst].set(tiles, mode="drop")
    adjacency = adjacency.reshape(rows, cols * nodes, nodes)
    picked = [dot(pick_slab, adjacency[s]).astype(BF16) for s in range(rows)]

    degree_wide = jnp.broadcast_to(degree.astype(BF16)[:, None], (nodes, 128))
    known = dot(pick_own, jnp.concatenate([cotangent, degree_wide], axis=1)).astype(BF16)

    slab_features = jnp.concatenate(feature_parts, axis=0)
    part = dot(jnp.concatenate(picked, axis=1), slab_features)
    chosen = dot(pick_column, slab_features).astype(BF16)
    fixed = jnp.concatenate([chosen, known], axis=1)
    got = trade(jnp.concatenate([part[half:].astype(BF16), fixed[half:]], axis=1), "col", 1)
    part = part[:half] + got[:, :width].astype(F32)
    fixed = fixed[:half] + got[:, width:]
    sent = jnp.concatenate([part[share:].astype(BF16), fixed[share:]], axis=1)
    sent, picked = lax.optimization_barrier((sent, picked))
    got = trade(sent, "col", 2)
    own_columns = picked[0] + sum(trade(picked[s], "row", s) for s in range(1, rows))
    agg_sum = part[:share] + got[:, :width].astype(F32)
    fixed = fixed[:share] + got[:, width:]
    feature_slots = fixed[:, :width]
    cotangent_slots = fixed[:, width : 2 * width]
    degree_slots = fixed[:, 2 * width :]
    degree_one = degree_slots[:, :1].astype(F32)
    inverse = jnp.where(degree_one > 0, 1.0 / jnp.maximum(degree_one, 1.0), 0.0)
    aggregate = (agg_sum * inverse).astype(BF16)
    before = dot(feature_slots, w_self) + dot(aggregate, w_neigh) + layer_bias
    slope = (cotangent_slots.astype(F32) * gelu_slope(before)).astype(BF16)

    found = jnp.concatenate([slope, aggregate, degree_slots], axis=1)
    found, feature_parts = lax.optimization_barrier((found, feature_parts))
    found = found + trade(found, "row", 2)
    found = found + trade(found, "row", 1)

    dense = sum(dot(adjacency[s], feature_parts[s]) for s in range(rows))
    middle = 2 * nodes
    dense = dense[:middle] + trade(dense[middle:].astype(BF16), "col", 1).astype(F32)
    own_sum = dense[:nodes] + trade(dense[nodes:].astype(BF16), "col", 2).astype(F32)

    everything = jnp.concatenate([found, feature_slots], axis=1)
    everything = jnp.concatenate([everything, trade(everything, "col", 2)], axis=0)
    everything = jnp.concatenate([everything, trade(everything, "col", 1)], axis=0)
    own_aggregate = (own_sum * (1.0 / degree.astype(F32))[:, None]).astype(BF16)
    own_before = dot(features, w_self) + dot(own_aggregate, w_neigh) + layer_bias
    hidden = gelu_value(own_before).astype(BF16)

    slope_all = everything[:, :width]
    aggregate_all = everything[:, width : 2 * width]
    degree_all = everything[:, 2 * width : 2 * width + 1].astype(F32)
    feature_all = everything[:, -width:]
    scale = 1.0 / math.sqrt(nodes * rows * cols)
    grad_self = dot(feature_all, slope_all, ((0,), (0,))) * scale
    grad_neigh = dot(aggregate_all, slope_all, ((0,), (0,))) * scale
    grad_bias = jnp.sum(slope_all.astype(F32), axis=0) * scale
    message = (dot(slope_all, w_neigh, ((1,), (1,))) / degree_all).astype(BF16)
    own_slope = dot(pick_own, slope_all, ((0,), (0,))).astype(BF16)
    grad_features = dot(own_slope, w_self, ((1,), (1,))) + dot(own_columns, message, ((0,), (0,)))
    return (hidden, grad_features.astype(BF16), grad_self, grad_neigh, grad_bias)


def tile_sum(values, take_index, put_index, usable, source, out_tiles, transpose, first_tile):
    slot_count, tile_width = (values.shape[0], values.shape[1])
    columns = source.shape[1]
    blocks = source.reshape(-1, tile_width, columns)
    group_size = math.gcd(slot_count, 16)
    pattern = "kji,kjf->kif" if transpose else "kij,kjf->kif"

    def advance(running, offset):
        tile_block = lax.dynamic_slice_in_dim(values, offset, group_size, 0)
        taken = lax.dynamic_slice_in_dim(take_index, offset, group_size, 0)
        placed = lax.dynamic_slice_in_dim(put_index, offset, group_size, 0) - first_tile
        allowed = lax.dynamic_slice_in_dim(usable, offset, group_size, 0)
        inside = allowed & (placed >= 0) & (placed < out_tiles)
        chosen = blocks[taken]
        product = jnp.einsum(pattern, tile_block, chosen, preferred_element_type=jnp.float32)
        product = product * inside.astype(jnp.float32)[:, None, None]
        where_to = jnp.where(inside, placed, 0)
        running = running.at[where_to].add(product)
        return (running, None)

    offsets = jnp.arange(0, slot_count, group_size, dtype=jnp.int32)
    running, _ = lax.scan(
        advance, jnp.zeros((out_tiles, tile_width, columns), jnp.float32), offsets
    )
    return running.reshape(out_tiles * tile_width, columns)


def dense_device(
    features,
    w_self,
    w_neigh,
    layer_bias,
    tile_vals,
    tile_dst,
    tile_src,
    tile_count,
    degree,
    target_ids,
    cotangent,
):
    row_count = lax.axis_size("row")
    col_count = lax.axis_size("col")
    node_rows = features.shape[0]
    tile_width = tile_vals.shape[-1]
    cell_tiles = tile_vals[0, 0]
    cell_dst = tile_dst[0, 0]
    cell_src = tile_src[0, 0]
    usable = jnp.arange(cell_tiles.shape[0], dtype=jnp.int32) < tile_count[0, 0]
    source = lax.all_gather(features, "row", axis=0, tiled=True)
    partial_value = tile_sum(
        cell_tiles,
        cell_src,
        cell_dst,
        usable,
        source,
        col_count * node_rows // tile_width,
        False,
        0,
    )
    agg_sum = lax.psum_scatter(partial_value, "col", scatter_dimension=0, tiled=True)
    inv_degree = 1.0 / degree.astype(jnp.float32)
    aggregate = (agg_sum * inv_degree[:, None]).astype(jnp.bfloat16)
    before = (
        jnp.dot(features, w_self, preferred_element_type=jnp.float32)
        + jnp.dot(aggregate, w_neigh, preferred_element_type=jnp.float32)
        + layer_bias
    )
    hidden = gelu_value(before).astype(jnp.bfloat16)
    first_node = (lax.axis_index("row") * col_count + lax.axis_index("col")) * node_rows
    node_ids = first_node + jnp.arange(node_rows, dtype=jnp.int32)
    target = jnp.any(node_ids[:, None] == target_ids[None, :], axis=1).astype(jnp.float32)
    slope_grad = (cotangent.astype(jnp.float32) * target[:, None] * gelu_slope(before)).astype(
        jnp.bfloat16
    )
    grad_scale = 1.0 / math.sqrt(node_rows * row_count * col_count)
    contract_rows = (((0,), (0,)), ((), ()))
    self_term = lax.dot_general(
        features, slope_grad, contract_rows, preferred_element_type=jnp.float32
    )
    neigh_term = lax.dot_general(
        aggregate, slope_grad, contract_rows, preferred_element_type=jnp.float32
    )
    bias_term = jnp.sum(slope_grad.astype(jnp.float32), axis=0)
    self_sum, neigh_sum, bias_sum = lax.psum((self_term, neigh_term, bias_term), ("row", "col"))
    contract_out = (((1,), (1,)), ((), ()))
    message = (
        lax.dot_general(slope_grad, w_neigh, contract_out, preferred_element_type=jnp.float32)
        * inv_degree[:, None]
    ).astype(jnp.bfloat16)
    message_slab = lax.all_gather(message, "col", axis=0, tiled=True)
    back_part = tile_sum(
        cell_tiles,
        cell_dst,
        cell_src,
        usable,
        message_slab,
        row_count * node_rows // tile_width,
        True,
        0,
    )
    neighbour_grad = lax.psum_scatter(
        back_part.astype(jnp.bfloat16).astype(jnp.float32).astype(jnp.bfloat16),
        "row",
        scatter_dimension=0,
        tiled=True,
    ).astype(jnp.float32)
    direct = lax.dot_general(slope_grad, w_self, contract_out, preferred_element_type=jnp.float32)
    grad_features = (direct + neighbour_grad).astype(jnp.bfloat16)
    return (
        hidden,
        grad_features,
        self_sum * grad_scale,
        neigh_sum * grad_scale,
        bias_sum * grad_scale,
    )


def solution(mesh):
    in_specs = (
        P(("groups", "row", "col"), None),
        P(),
        P(),
        P(),
        P(("groups", "row"), "col", None, None, None),
        P(("groups", "row"), "col", None),
        P(("groups", "row"), "col", None),
        P(("groups", "row"), "col"),
        P(("groups", "row", "col")),
        P("groups"),
        P(("groups", "row", "col"), None),
    )
    out_specs = (
        P(("groups", "row", "col"), None),
        P(("groups", "row", "col"), None),
        P("groups", None),
        P("groups", None),
        P("groups"),
    )
    parts = mesh.shape["row"] * mesh.shape["col"]
    per_device = compact_device if parts <= 16 else dense_device
    return jax.shard_map(
        per_device, mesh=mesh, in_specs=in_specs, out_specs=out_specs, check_vma=False
    )
```

```python
import functools
import itertools
import math

import jax
import jax.numpy as jnp
from jax import lax
from jax.experimental import pallas as pl
from jax.experimental.pallas import tpu as pltpu
from jax.sharding import PartitionSpec as P

F32 = jnp.float32
BF16 = jnp.bfloat16


def gelu_value(inputs):
    return 0.5 * inputs * (1.0 + jax.scipy.special.erf(inputs * 0.7071067811865476))


def gelu_slope(inputs):
    return (
        0.5 * (1.0 + jax.scipy.special.erf(inputs * 0.7071067811865476))
        + inputs * jnp.exp(-0.5 * inputs * inputs) * 0.3989422804014327
    )


def dot(left, right, dims=((1,), (0,))):
    return lax.dot_general(left, right, (dims, ((), ())), preferred_element_type=F32)


def trade(block, axis, step):
    return lax.ppermute(block, axis, [(i, i ^ step) for i in range(lax.axis_size(axis))])


def flip(pair, axis, bit):
    return jnp.where(bit == 1, jnp.flip(pair, axis), pair)


def call(kernel, outputs, *inputs, spaces=(), scratch=()):
    inputs = [
        pltpu.with_memory_space_constraint(x, y) if y == pltpu.HBM else x
        for x, y in itertools.zip_longest(inputs, spaces)
    ]
    spaces = list(spaces) + [pltpu.VMEM] * (len(inputs) - len(spaces))
    return pl.pallas_call(
        kernel,
        out_shape=[jax.ShapeDtypeStruct(shape, dtype) for shape, dtype in outputs],
        in_specs=[pl.BlockSpec(memory_space=space) for space in spaces],
        out_specs=[pl.BlockSpec(memory_space=pltpu.VMEM) for _ in outputs],
        scratch_shapes=scratch,
        compiler_params=pltpu.CompilerParams(vmem_limit_bytes=32 * 2**20),
    )(*inputs)


def spread(block, axis):
    return [trade(block, axis, step) for step in range(lax.axis_size(axis) - 1, 0, -1)]


def swap_bits(index):
    return index // 2 + index % 2 * 2


def select(rows, cols, ids_in, src_in, dst_in, count_in, tiles_in, cotangent_in, degree_in, *refs):
    weights_in, refs = refs[:3], refs[3:]
    adjacency, column_picks, own_picks, known = refs[:4]
    picked, refs = refs[4 : 4 + rows], refs[4 + rows :]
    weights, (picks, src, dst, count, tiles, cotangent, degree, ids, sems) = refs[:3], refs[3:]
    pairs = [(src_in, src), (dst_in, dst), (count_in, count), (tiles_in, tiles)]
    pairs += [(cotangent_in, cotangent), (degree_in, degree), (ids_in, ids)]
    pairs += list(zip(weights_in, weights))
    copies = [pltpu.make_async_copy(a, b, sems.at[i]) for i, (a, b) in enumerate(pairs)]
    for copy in copies:
        copy.start()
    row, col = lax.axis_index("row"), lax.axis_index("col")
    share, nodes, width = ids.shape[1], cotangent.shape[0], cotangent.shape[1]
    slots = share * cols
    adjacency[...] = jnp.zeros(adjacency.shape, adjacency.dtype)
    for copy in copies[:7]:
        copy.wait()
    for k in range(tiles.shape[2]):

        @pl.when(k < count[0, 0])
        def _():
            down = pl.multiple_of(swap_bits(dst[0, 0, k] ^ col) * nodes, nodes)
            adjacency[src[0, 0, k] ^ row, pl.ds(down, nodes), :] = tiles[0, 0, k]

    lanes = lax.broadcasted_iota(jnp.int32, (share, nodes), 1)
    across = lax.broadcasted_iota(jnp.int32, (nodes, share), 0)
    for p in range(cols):
        here = pl.ds(p * share, share)
        line = jnp.broadcast_to(ids[pl.ds(col ^ swap_bits(p), 1), :], (nodes, share))
        stack = line.T
        for k in range(cols):
            base = (row * cols + (col ^ swap_bits(k))) * nodes
            picks[here, k * nodes : (k + 1) * nodes] = (stack == lanes + base).astype(BF16)
        for s in range(rows):
            base = ((row ^ s) * cols + col) * nodes
            column_picks[here, s * nodes : (s + 1) * nodes] = (stack == lanes + base).astype(BF16)
        base = (row * cols + col) * nodes
        own_picks[:, here] = (line == across + base).astype(BF16)
    for s in range(rows):
        picked[s][...] = dot(picks[...], adjacency[s]).astype(BF16)
    own = picks[:, :nodes]
    known[:, :width] = dot(own, cotangent[...]).astype(BF16)
    for copy in copies[7:]:
        copy.wait()
    counts = degree[...].astype(F32)
    counts = jnp.sum(own.astype(F32) * counts, axis=1, keepdims=True)
    known[:, width:] = jnp.broadcast_to(counts, (slots, 128)).astype(BF16)


def combine(rows, *refs):
    column_picks, known, *rest = refs
    features, picked = rest[:rows][::-1], rest[rows : 2 * rows]
    sent, part, fixed = rest[2 * rows :]
    nodes, width = features[0].shape
    half = part.shape[0]
    sums = sum(dot(picked[s][...], features[s][...]) for s in range(rows))
    chosen = sum(
        dot(column_picks[:, s * nodes : (s + 1) * nodes], features[s][...]) for s in range(rows)
    ).astype(BF16)
    part[...] = sums[:half]
    fixed[:, :width] = chosen[:half]
    fixed[:, width:] = known[:half, :]
    sent[:, :width] = sums[half:].astype(BF16)
    sent[:, width : 2 * width] = chosen[half:]
    sent[:, 2 * width :] = known[half:, :]


def relay(part, fixed, got, sent, part_out, fixed_out):
    share, width = part_out.shape
    sums = part[...] + got[:, :width].astype(F32)
    rest = fixed[...] + got[:, width:]
    part_out[...] = sums[:share]
    fixed_out[...] = rest[:share]
    sent[:, :width] = sums[share:].astype(BF16)
    sent[:, width:] = rest[share:]


def slopes(part, fixed, got, w_self, w_neigh, layer_bias, found, features):
    width = part.shape[1]
    total = part[...] + got[:, :width].astype(F32)
    rest = fixed[...] + got[:, width:]
    features[...] = rest[:, :width]
    cotangent = rest[:, width : 2 * width].astype(F32)
    degrees = rest[:, 2 * width :]
    degree = degrees[:, :1].astype(F32)
    inverse = jnp.where(degree > 0, 1.0 / jnp.maximum(degree, 1.0), 0.0)
    aggregate = (total * inverse).astype(BF16)
    before = dot(rest[:, :width], w_self[...]) + dot(aggregate, w_neigh[...]) + layer_bias[...]
    found[:, :width] = (cotangent * gelu_slope(before)).astype(BF16)
    found[:, width : 2 * width] = aggregate
    found[:, 2 * width :] = degrees


def merge(*refs):
    *parts, features, everything = refs
    width = features.shape[1]
    everything[:, :-width] = sum(part[...] for part in parts)
    everything[:, -width:] = features[...]


def finish(scale, mine, other, own_columns, own_picks, w_self, w_neigh, *outs):
    grad_features, grad_self, grad_neigh, grad_bias = outs
    width = w_self.shape[0]
    half = mine.shape[0]
    front, back = ((0,), (0,)), ((1,), (1,))
    slope = [mine[:, :width], other[:, :width]]
    both = (mine, other)
    pairs = list(zip(both, slope))
    grad_self[...] = sum(dot(e[:, -width:], g, front) for e, g in pairs) * scale
    grad_neigh[...] = sum(dot(e[:, width : 2 * width], g, front) for e, g in pairs) * scale
    grad_bias[...] = sum(jnp.sum(g.astype(F32), axis=0, keepdims=True) for g in slope) * scale
    own_slope = dot(own_picks[:, :half], slope[0]) + dot(own_picks[:, half:], slope[1])
    total = dot(own_slope.astype(BF16), w_self[...], back)
    for j, (e, g) in enumerate(pairs):
        degree = e[:, 2 * width : 2 * width + 1].astype(F32)
        message = (dot(g, w_neigh[...], back) / degree).astype(BF16)
        total += dot(own_columns[j * half : (j + 1) * half, :], message, front)
    grad_features[...] = total.astype(BF16)


def compact_device(
    features,
    w_self,
    w_neigh,
    layer_bias,
    tile_vals,
    tile_dst,
    tile_src,
    tile_count,
    degree,
    target_ids,
    cotangent,
):
    rows = lax.axis_size("row")
    cols = lax.axis_size("col")
    nodes, width = features.shape
    slots = target_ids.shape[0]
    share = slots // cols
    half = slots // 2

    feature_parts = spread(features, "row") + [features]

    bias = layer_bias.reshape(1, width)
    adjacency, column_picks, own_picks, known, *picked = call(
        functools.partial(select, rows, cols),
        [
            ((rows, cols * nodes, nodes), BF16),
            ((slots, rows * nodes), BF16),
            ((nodes, slots), BF16),
            ((slots, width + 128), BF16),
        ]
        + [((slots, nodes), BF16)] * rows
        + [((width, width), BF16)] * 2
        + [((1, width), F32)],
        target_ids.reshape(cols, share),
        tile_src,
        tile_dst,
        tile_count,
        tile_vals,
        cotangent,
        degree.reshape(1, nodes),
        w_self,
        w_neigh,
        bias,
        spaces=[pl.ANY] + [pltpu.HBM] * 2 + [pl.ANY] + [pltpu.HBM] * 6,
        scratch=[pltpu.VMEM((slots, cols * nodes), BF16)]
        + [pltpu.SMEM(x.shape, x.dtype) for x in (tile_src, tile_dst, tile_count)]
        + [pltpu.VMEM(x.shape, x.dtype) for x in (tile_vals, cotangent)]
        + [pltpu.VMEM((1, nodes), jnp.int32), pltpu.VMEM((cols, share), jnp.int32)]
        + [pltpu.SemaphoreType.DMA((10,))],
    )
    *picked, w_self, w_neigh, bias = picked
    own_columns = sum(trade(picked[s], "row", s) for s in range(rows - 1, 0, -1)) + picked[0]
    sent, part, fixed = call(
        functools.partial(combine, rows),
        [((half, 2 * width + width + 128), BF16), ((half, width), F32), ((half, 2 * width + 128), BF16)],
        column_picks,
        known,
        *feature_parts,
        *picked,
    )
    got = trade(sent, "col", 1)
    sent, part, fixed = call(
        relay,
        [((share, 3 * width + 128), BF16), ((share, width), F32), ((share, 2 * width + 128), BF16)],
        part,
        fixed,
        got,
    )
    sent, feature_parts = lax.optimization_barrier((sent, feature_parts))
    got = trade(sent, "col", 2)
    found, feature_slots = call(
        slopes,
        [((share, 2 * width + 128), BF16), ((share, width), BF16)],
        part,
        fixed,
        got,
        w_self,
        w_neigh,
        bias,
    )
    (everything,) = call(
        merge, [((share, 3 * width + 128), BF16)], *spread(found, "row"), found, feature_slots
    )

    dense = sum(dot(adjacency[s], feature_parts[-1 - s]) for s in range(rows))
    middle = 2 * nodes
    dense = dense[:middle] + trade(dense[middle:].astype(BF16), "col", 1).astype(F32)
    own_sum = dense[:nodes] + trade(dense[nodes:].astype(BF16), "col", 2).astype(F32)

    everything = jnp.concatenate([everything, trade(everything, "col", 2)], axis=0)
    other = trade(everything, "col", 1)
    own_aggregate = (own_sum * (1.0 / degree.astype(F32))[:, None]).astype(BF16)
    own_before = dot(features, w_self) + dot(own_aggregate, w_neigh) + bias
    hidden = gelu_value(own_before).astype(BF16)

    grad_features, grad_self, grad_neigh, grad_bias = call(
        functools.partial(finish, 1.0 / math.sqrt(nodes * rows * cols)),
        [((nodes, width), BF16), ((width, width), F32), ((width, width), F32), ((1, width), F32)],
        everything,
        other,
        own_columns,
        own_picks,
        w_self,
        w_neigh,
    )
    return (hidden, grad_features, grad_self, grad_neigh, grad_bias.reshape(width))


def tile_sum(values, take_index, put_index, usable, source, out_tiles, transpose, first_tile):
    slot_count, tile_width = (values.shape[0], values.shape[1])
    columns = source.shape[1]
    blocks = source.reshape(-1, tile_width, columns)
    group_size = math.gcd(slot_count, 16)
    pattern = "kji,kjf->kif" if transpose else "kij,kjf->kif"

    def advance(running, offset):
        tile_block = lax.dynamic_slice_in_dim(values, offset, group_size, 0)
        taken = lax.dynamic_slice_in_dim(take_index, offset, group_size, 0)
        placed = lax.dynamic_slice_in_dim(put_index, offset, group_size, 0) - first_tile
        allowed = lax.dynamic_slice_in_dim(usable, offset, group_size, 0)
        inside = allowed & (placed >= 0) & (placed < out_tiles)
        chosen = blocks[taken]
        product = jnp.einsum(pattern, tile_block, chosen, preferred_element_type=jnp.float32)
        product = product * inside.astype(jnp.float32)[:, None, None]
        where_to = jnp.where(inside, placed, 0)
        running = running.at[where_to].add(product)
        return (running, None)

    offsets = jnp.arange(0, slot_count, group_size, dtype=jnp.int32)
    running, _ = lax.scan(
        advance, jnp.zeros((out_tiles, tile_width, columns), jnp.float32), offsets
    )
    return running.reshape(out_tiles * tile_width, columns)


def dense_device(
    features,
    w_self,
    w_neigh,
    layer_bias,
    tile_vals,
    tile_dst,
    tile_src,
    tile_count,
    degree,
    target_ids,
    cotangent,
):
    row_count = lax.axis_size("row")
    col_count = lax.axis_size("col")
    node_rows = features.shape[0]
    tile_width = tile_vals.shape[-1]
    cell_tiles = tile_vals[0, 0]
    cell_dst = tile_dst[0, 0]
    cell_src = tile_src[0, 0]
    usable = jnp.arange(cell_tiles.shape[0], dtype=jnp.int32) < tile_count[0, 0]
    source = lax.all_gather(features, "row", axis=0, tiled=True)
    partial_value = tile_sum(
        cell_tiles,
        cell_src,
        cell_dst,
        usable,
        source,
        col_count * node_rows // tile_width,
        False,
        0,
    )
    agg_sum = lax.psum_scatter(partial_value, "col", scatter_dimension=0, tiled=True)
    inv_degree = 1.0 / degree.astype(jnp.float32)
    aggregate = (agg_sum * inv_degree[:, None]).astype(jnp.bfloat16)
    before = (
        jnp.dot(features, w_self, preferred_element_type=jnp.float32)
        + jnp.dot(aggregate, w_neigh, preferred_element_type=jnp.float32)
        + layer_bias
    )
    hidden = gelu_value(before).astype(jnp.bfloat16)
    first_node = (lax.axis_index("row") * col_count + lax.axis_index("col")) * node_rows
    node_ids = first_node + jnp.arange(node_rows, dtype=jnp.int32)
    target = jnp.any(node_ids[:, None] == target_ids[None, :], axis=1).astype(jnp.float32)
    slope_grad = (cotangent.astype(jnp.float32) * target[:, None] * gelu_slope(before)).astype(
        jnp.bfloat16
    )
    grad_scale = 1.0 / math.sqrt(node_rows * row_count * col_count)
    contract_rows = (((0,), (0,)), ((), ()))
    self_term = lax.dot_general(
        features, slope_grad, contract_rows, preferred_element_type=jnp.float32
    )
    neigh_term = lax.dot_general(
        aggregate, slope_grad, contract_rows, preferred_element_type=jnp.float32
    )
    bias_term = jnp.sum(slope_grad.astype(jnp.float32), axis=0)
    self_sum, neigh_sum, bias_sum = lax.psum((self_term, neigh_term, bias_term), ("row", "col"))
    contract_out = (((1,), (1,)), ((), ()))
    message = (
        lax.dot_general(slope_grad, w_neigh, contract_out, preferred_element_type=jnp.float32)
        * inv_degree[:, None]
    ).astype(jnp.bfloat16)
    message_slab = lax.all_gather(message, "col", axis=0, tiled=True)
    back_part = tile_sum(
        cell_tiles,
        cell_dst,
        cell_src,
        usable,
        message_slab,
        row_count * node_rows // tile_width,
        True,
        0,
    )
    neighbour_grad = lax.psum_scatter(
        back_part.astype(jnp.bfloat16).astype(jnp.float32).astype(jnp.bfloat16),
        "row",
        scatter_dimension=0,
        tiled=True,
    ).astype(jnp.float32)
    direct = lax.dot_general(slope_grad, w_self, contract_out, preferred_element_type=jnp.float32)
    grad_features = (direct + neighbour_grad).astype(jnp.bfloat16)
    return (
        hidden,
        grad_features,
        self_sum * grad_scale,
        neigh_sum * grad_scale,
        bias_sum * grad_scale,
    )


def solution(mesh):
    in_specs = (
        P(("groups", "row", "col"), None),
        P(),
        P(),
        P(),
        P(("groups", "row"), "col", None, None, None),
        P(("groups", "row"), "col", None),
        P(("groups", "row"), "col", None),
        P(("groups", "row"), "col"),
        P(("groups", "row", "col")),
        P("groups"),
        P(("groups", "row", "col"), None),
    )
    out_specs = (
        P(("groups", "row", "col"), None),
        P(("groups", "row", "col"), None),
        P("groups", None),
        P("groups", None),
        P("groups"),
    )
    parts = mesh.shape["row"] * mesh.shape["col"]
    per_device = compact_device if parts <= 16 else dense_device
    return jax.shard_map(
        per_device, mesh=mesh, in_specs=in_specs, out_specs=out_specs, check_vma=False
    )
```

```python
import functools
import itertools
import math

import jax
import jax.numpy as jnp
from jax import lax
from jax.experimental import pallas as pl
from jax.experimental.pallas import tpu as pltpu
from jax.sharding import PartitionSpec as P

F32 = jnp.float32
BF16 = jnp.bfloat16


def gelu_value(inputs):
    return 0.5 * inputs * (1.0 + jax.scipy.special.erf(inputs * 0.7071067811865476))


def gelu_slope(inputs):
    return (
        0.5 * (1.0 + jax.scipy.special.erf(inputs * 0.7071067811865476))
        + inputs * jnp.exp(-0.5 * inputs * inputs) * 0.3989422804014327
    )


def dot(left, right, dims=((1,), (0,))):
    return lax.dot_general(left, right, (dims, ((), ())), preferred_element_type=F32)


def trade(block, axis, step):
    return lax.ppermute(block, axis, [(i, i ^ step) for i in range(lax.axis_size(axis))])


def swap_quarters(line):
    first, second, third, last = jnp.split(line, 4, axis=1)
    return jnp.concatenate([first, third, second, last], axis=1)


def flip(line, parts, bit):
    cut = jnp.split(line, parts, axis=1)
    turned = [cut[i ^ 1] for i in range(parts)]
    return jnp.where(bit == 1, jnp.concatenate(turned, axis=1), line)


def call(kernel, outputs, *inputs, spaces=(), scratch=(), out_space=pltpu.VMEM, cost=0):
    inputs = [
        pltpu.with_memory_space_constraint(x, y) if y == pltpu.HBM else x
        for x, y in itertools.zip_longest(inputs, spaces)
    ]
    spaces = list(spaces) + [pltpu.VMEM] * (len(inputs) - len(spaces))
    return pl.pallas_call(
        kernel,
        out_shape=[jax.ShapeDtypeStruct(shape, dtype) for shape, dtype in outputs],
        in_specs=[pl.BlockSpec(memory_space=space) for space in spaces],
        out_specs=[pl.BlockSpec(memory_space=out_space) for _ in outputs],
        scratch_shapes=scratch,
        cost_estimate=pl.CostEstimate(flops=int(cost * 1e9), bytes_accessed=0, transcendentals=0) if cost else None,
        compiler_params=pltpu.CompilerParams(vmem_limit_bytes=32 * 2**20),
    )(*inputs)


CFG = {'forder': [2, 3, 1], 'split': True, 'halves': [0, 2, 1, 3], 'a1': 'none', 'a2': 'none', 'dd': 'sent', 'p3d': True, 'p3': [3, 1, 2], 'p3split': False, 'fp': 'found1', 'dx': 'found1', 'hid': 'none', 'cd': 3}


def spread(block, axis, steps):
    return {step: trade(block, axis, step) for step in steps}


def swap_bits(index):
    return index // 2 + index % 2 * 2


def select(rows, cols, ids_in, src_in, dst_in, count_in, tiles_in, cotangent_in, degree_in, *refs):
    weights_in, refs = refs[:3], refs[3:]
    adjacency, column_picks, own_picks, known, near, far, inverse, *refs = refs
    weights, (picks, src, dst, count, tiles, cotangent, degree, ids, sems) = refs[:3], refs[3:]
    pairs = [(src_in, src), (dst_in, dst), (count_in, count), (tiles_in, tiles)]
    pairs += [(cotangent_in, cotangent), (degree_in, degree), (ids_in, ids)]
    pairs += list(zip(weights_in, weights))
    copies = [pltpu.make_async_copy(a, b, sems.at[i]) for i, (a, b) in enumerate(pairs)]
    for copy in copies:
        copy.start()
    row, col = lax.axis_index("row"), lax.axis_index("col")
    slots, (nodes, width) = ids.shape[1], cotangent.shape
    adjacency[...] = jnp.zeros(adjacency.shape, adjacency.dtype)
    for copy in copies[:7]:
        copy.wait()
    for k in range(tiles.shape[2]):

        @pl.when(k < count[0, 0])
        def _():
            down = pl.multiple_of(swap_bits(dst[0, 0, k] ^ col) * nodes, nodes)
            adjacency[src[0, 0, k] ^ row, pl.ds(down, nodes), :] = tiles[0, 0, k]

    line = flip(flip(swap_quarters(ids[...]), 2, col % 2), 4, col // 2)
    line = jnp.broadcast_to(line, (nodes, slots))
    stack = line.T
    lanes = lax.broadcasted_iota(jnp.int32, (slots, nodes), 1)
    for k in range(cols):
        base = (row * cols + (col ^ swap_bits(k))) * nodes
        picks[:, k * nodes : (k + 1) * nodes] = (stack == lanes + base).astype(BF16)
    for s in range(rows):
        base = ((row ^ s) * cols + col) * nodes
        column_picks[:, s * nodes : (s + 1) * nodes] = (stack == lanes + base).astype(BF16)
    base = (row * cols + col) * nodes
    across = lax.broadcasted_iota(jnp.int32, (nodes, slots), 0)
    own_picks[...] = (line == across + base).astype(BF16)
    for s in range(rows):
        block = dot(picks[...], adjacency[s]).astype(BF16)
        index = list(CFG["halves"]).index(s)
        (far if index // 2 else near)[index % 2 * slots : (index % 2 + 1) * slots, :] = block
    own = picks[:, :nodes]
    known[:, :width] = dot(own, cotangent[...]).astype(BF16)
    for copy in copies[7:]:
        copy.wait()
    counts = degree[...].astype(F32)
    inverse[...] = 1.0 / jnp.broadcast_to(counts, (nodes, nodes)).T
    counts = jnp.sum(own.astype(F32) * counts, axis=1, keepdims=True)
    known[:, width:] = jnp.broadcast_to(counts, (slots, 128)).astype(BF16)


def block_of(step, near, far, slots):
    index = list(CFG["halves"]).index(step)
    return (far if index // 2 else near)[index % 2 * slots : (index % 2 + 1) * slots, :]


def dense_part(steps, adjacency, *refs):
    *features, kept, sent = refs
    total = sum(dot(adjacency[step], block[...]) for step, block in zip(steps, features))
    half = kept.shape[0]
    kept[...] = total[:half]
    sent[...] = total[half:].astype(BF16)


def begin(step, column_picks, features, near, far, total, chosen):
    slots, nodes = column_picks.shape[0], features.shape[0]
    total[...] = dot(block_of(step, near, far, slots), features[...])
    chosen[...] = dot(column_picks[:, step * nodes : (step + 1) * nodes], features[...])


def combine(steps, column_picks, known, *refs):
    features, (near, far, *first, sent, part, fixed) = refs[: len(steps)], refs[len(steps) :]
    nodes, width = features[0].shape
    half = part.shape[0]
    sums, picked = [x[...] for x in first] or [0.0, 0.0]
    for step, block in zip(steps, features):
        sums += dot(block_of(step, near, far, 2 * half), block[...])
        picked += dot(column_picks[:, step * nodes : (step + 1) * nodes], block[...])
    picked = picked.astype(BF16)
    part[...] = sums[:half]
    fixed[:, :width] = picked[:half]
    fixed[:, width:] = known[:half, :]
    sent[:, :width] = sums[half:].astype(BF16)
    sent[:, width : 2 * width] = picked[half:]
    sent[:, 2 * width :] = known[half:, :]


def relay(part, fixed, got, sent, part_out, fixed_out):
    share, width = part_out.shape
    sums = part[...] + got[:, :width].astype(F32)
    rest = fixed[...] + got[:, width:]
    part_out[...] = sums[:share]
    fixed_out[...] = rest[:share]
    sent[:, :width] = sums[share:].astype(BF16)
    sent[:, width:] = rest[share:]


def slopes(part, fixed, got, w_self, w_neigh, layer_bias, found, features):
    width = part.shape[1]
    total = part[...] + got[:, :width].astype(F32)
    rest = fixed[...] + got[:, width:]
    features[...] = rest[:, :width]
    cotangent = rest[:, width : 2 * width].astype(F32)
    degrees = rest[:, 2 * width :]
    degree = degrees[:, :1].astype(F32)
    inverse = jnp.where(degree > 0, 1.0 / jnp.maximum(degree, 1.0), 0.0)
    aggregate = (total * inverse).astype(BF16)
    before = dot(rest[:, :width], w_self[...]) + dot(aggregate, w_neigh[...]) + layer_bias[...]
    slope = (cotangent * gelu_slope(before)).astype(BF16)
    share, bands = part.shape[0], width // 128
    for b in range(bands):
        found[b * share : (b + 1) * share, :] = slope[:, b * 128 : (b + 1) * 128]
        down = (bands + b) * share
        found[down : down + share, :] = aggregate[:, b * 128 : (b + 1) * 128]
    line = degrees.astype(F32).T[:16, :]
    line = jnp.concatenate([line, jnp.zeros((16, 128 - share), F32)], axis=1)
    found[2 * bands * share :, :] = line.astype(BF16)


def merge(*refs):
    refs[-1][...] = sum(part[...] for part in refs[:-1])


def activate(features, total, got, inverse, w_self, w_neigh, layer_bias, hidden):
    total = total[...] + got[...].astype(F32)
    aggregate = (total * inverse[:, :1]).astype(BF16)
    before = dot(features[...], w_self[...]) + dot(aggregate, w_neigh[...]) + layer_bias[...]
    hidden[...] = gelu_value(before).astype(BF16)


def finish(scale, *refs):
    found, features, refs = refs[:2], refs[2:4], refs[4:]
    own_columns, own_picks, w_self, w_neigh, *refs = refs
    outs, (slope, aggregate, *results, sems) = refs[:4], refs[4:]
    grad_features, grad_self, grad_neigh, grad_bias = results
    slots, width = slope.shape
    half, bands = slots // 2, width // 128
    share = half // 2
    size = found[0].shape[0] // 2
    front, back = ((0,), (0,)), ((1,), (1,))
    degrees = []
    for q in range(4):
        part, base, here = found[q // 2], q % 2 * size, slice(q * share, (q + 1) * share)
        for b in range(bands):
            lanes = slice(b * 128, (b + 1) * 128)
            slope[here, lanes] = part[base + b * share : base + (b + 1) * share, :]
            down = base + (bands + b) * share
            aggregate[here, lanes] = part[down : down + share, :]
        degrees.append(part[base + size - 16 : base + size, :].astype(F32)[:1, :share])
    copies = [pltpu.make_async_copy(a, b, sems.at[i]) for i, (a, b) in enumerate(zip(results, outs))]
    grad_self[...] = scale * (
        dot(features[0][...], slope[:half, :], front)
        + dot(features[1][...], slope[half:, :], front)
    )
    copies[1].start()
    grad_neigh[...] = dot(aggregate[...], slope[...], front) * scale
    copies[2].start()
    grad_bias[...] = jnp.sum(slope[...].astype(F32), axis=0, keepdims=True) * scale
    copies[3].start()
    degree = jnp.broadcast_to(jnp.concatenate(degrees, axis=1), (128, slots)).T[:, :1]
    message = (dot(slope[...], w_neigh[...], back) / degree).astype(BF16)
    own_slope = dot(own_picks[...], slope[...]).astype(BF16)
    total = dot(own_slope, w_self[...], back) + dot(own_columns[...], message, front)
    grad_features[...] = total.astype(BF16)
    copies[0].start()
    for copy in copies:
        copy.wait()


def compact_device(
    features,
    w_self,
    w_neigh,
    layer_bias,
    tile_vals,
    tile_dst,
    tile_src,
    tile_count,
    degree,
    target_ids,
    cotangent,
):
    rows = lax.axis_size("row")
    cols = lax.axis_size("col")
    nodes, width = features.shape
    slots = target_ids.shape[0]
    share = slots // cols
    half = slots // 2

    tie = lax.optimization_barrier
    feature_parts = spread(features, "row", CFG["forder"])
    steps = tuple(feature_parts)
    feature_parts[0] = features

    bias = layer_bias.reshape(1, width)
    adjacency, column_picks, own_picks, known, near, far, inverse, w_self, w_neigh, bias = call(
        functools.partial(select, rows, cols),
        [
            ((rows, cols * nodes, nodes), BF16),
            ((slots, rows * nodes), BF16),
            ((nodes, slots), BF16),
            ((slots, width + 128), BF16),
        ]
        + [((rows // 2 * slots, nodes), BF16)] * 2
        + [((nodes, nodes), F32)]
        + [((width, width), BF16)] * 2
        + [((1, width), F32)],
        target_ids.reshape(1, slots),
        tile_src,
        tile_dst,
        tile_count,
        tile_vals,
        cotangent,
        degree.reshape(1, nodes),
        w_self,
        w_neigh,
        bias,
        spaces=[pltpu.HBM] * 3 + [pl.ANY] + [pltpu.HBM] * 6,
        scratch=[pltpu.VMEM((slots, cols * nodes), BF16)]
        + [pltpu.SMEM(x.shape, x.dtype) for x in (tile_src, tile_dst, tile_count)]
        + [pltpu.VMEM(x.shape, x.dtype) for x in (tile_vals, cotangent)]
        + [pltpu.VMEM((1, nodes), jnp.int32), pltpu.VMEM((1, slots), jnp.int32)]
        + [pltpu.SemaphoreType.DMA((10,))],
    )
    first = ()
    if CFG["split"]:
        first = call(
            functools.partial(begin, steps[0]),
            [((slots, width), F32)] * 2,
            column_picks,
            feature_parts[steps[0]],
            near,
            far,
        )
    later = steps[len(first) // 2 :] + (0,)
    sent, part, fixed = call(
        functools.partial(combine, later),
        [((half, 3 * width + 128), BF16), ((half, width), F32), ((half, 2 * width + 128), BF16)],
        column_picks,
        known,
        *[feature_parts[step] for step in later],
        near,
        far,
        *first,
    )
    got = trade(sent, "col", 1)
    sent, part, fixed = call(
        relay,
        [((share, 3 * width + 128), BF16), ((share, width), F32), ((share, 2 * width + 128), BF16)],
        part,
        fixed,
        got,
    )
    if CFG["a1"] == "sent":
        sent, far = tie((sent, far))
    if CFG["dd"] == "sent":
        sent, feature_parts = tie((sent, feature_parts))
    got = trade(sent, "col", 2)
    found, feature_slots = call(
        slopes,
        [((2 * (width // 128) * share + 16, 128), BF16), ((share, width), BF16)],
        part,
        fixed,
        got,
        w_self,
        w_neigh,
        bias,
    )
    if CFG["a1"] == "found":
        found, far = tie((found, far))
    if CFG["dd"] == "found":
        found, feature_parts = tie((found, feature_parts))
    near_step, far_step = CFG["halves"][1], CFG["halves"][2]
    columns = near + trade(far, "row", far_step)
    if CFG["a2"] == "found":
        found, columns = tie((found, columns))

    def prepare_dense(feature_parts):
        kept, dense = call(
            functools.partial(dense_part, steps + (0,)),
            [((2 * nodes, width), F32), ((2 * nodes, width), BF16)],
            adjacency,
            *[feature_parts[step] for step in steps + (0,)],
            cost=CFG["cd"],
        )
        return kept + trade(dense, "col", 1).astype(F32)

    dense = prepare_dense(feature_parts)
    parts = spread(found, "row", CFG["p3"]) if CFG["p3d"] else None
    if CFG["p3d"]:
        if CFG["p3split"]:
            (found,) = call(merge, [(found.shape, BF16)], parts.pop(CFG["p3"][0]), found)
    else:
        (found,) = call(merge, [(found.shape, BF16)], trade(found, "row", CFG["p3"][0]), found)
    if CFG["a2"] == "found1":
        found, columns = tie((found, columns))
    if CFG["fp"] == "found1":
        found, feature_slots = tie((found, feature_slots))
    if CFG["dx"] == "found1":
        found, dense = tie((found, dense))
    if CFG["p3d"]:
        (found,) = call(merge, [(found.shape, BF16)], *parts.values(), found)
    else:
        (found,) = call(merge, [(found.shape, BF16)], trade(found, "row", CFG["p3"][1]), found)
    if CFG["dx"] == "merged":
        found, dense = tie((found, dense))
    own_columns = columns[:slots] + trade(columns[slots:], "row", near_step)
    dense_got = trade(dense[nodes:].astype(BF16), "col", 2)
    if CFG["fp"] != "none":
        feature_mine = jnp.concatenate([feature_slots, trade(feature_slots, "col", 2)], axis=0)
        feature_other = trade(feature_mine, "col", 1)
        everything = found
    else:
        everything = jnp.concatenate([found, feature_slots], axis=1)
    found_mine = jnp.concatenate([everything, trade(everything, "col", 2)], axis=0)
    if CFG["hid"] == "mine":
        found_mine, dense_got = tie((found_mine, dense_got))
    found_other = trade(found_mine, "col", 1)
    if CFG["fp"] == "none":
        feature_mine, feature_other = found_mine[:, -width:], found_other[:, -width:]
    (hidden,) = call(
        activate,
        [((nodes, width), BF16)],
        features,
        dense[:nodes],
        dense_got,
        inverse,
        w_self,
        w_neigh,
        bias,
    )
    results = [((nodes, width), BF16), ((width, width), F32), ((width, width), F32), ((1, width), F32)]
    grad_features, grad_self, grad_neigh, grad_bias = call(
        functools.partial(finish, 1.0 / math.sqrt(nodes * rows * cols)),
        results,
        found_mine,
        found_other,
        feature_mine,
        feature_other,
        own_columns,
        own_picks,
        w_self,
        w_neigh,
        scratch=[pltpu.VMEM((slots, width), BF16)] * 2
        + [pltpu.VMEM(*result) for result in results]
        + [pltpu.SemaphoreType.DMA((4,))],
        out_space=pl.ANY,
    )
    return (hidden, grad_features, grad_self, grad_neigh, grad_bias.reshape(width))


def tile_sum(values, take_index, put_index, usable, source, out_tiles, transpose, first_tile):
    slot_count, tile_width = (values.shape[0], values.shape[1])
    columns = source.shape[1]
    blocks = source.reshape(-1, tile_width, columns)
    group_size = math.gcd(slot_count, 16)
    pattern = "kji,kjf->kif" if transpose else "kij,kjf->kif"

    def advance(running, offset):
        tile_block = lax.dynamic_slice_in_dim(values, offset, group_size, 0)
        taken = lax.dynamic_slice_in_dim(take_index, offset, group_size, 0)
        placed = lax.dynamic_slice_in_dim(put_index, offset, group_size, 0) - first_tile
        allowed = lax.dynamic_slice_in_dim(usable, offset, group_size, 0)
        inside = allowed & (placed >= 0) & (placed < out_tiles)
        chosen = blocks[taken]
        product = jnp.einsum(pattern, tile_block, chosen, preferred_element_type=jnp.float32)
        product = product * inside.astype(jnp.float32)[:, None, None]
        where_to = jnp.where(inside, placed, 0)
        running = running.at[where_to].add(product)
        return (running, None)

    offsets = jnp.arange(0, slot_count, group_size, dtype=jnp.int32)
    running, _ = lax.scan(
        advance, jnp.zeros((out_tiles, tile_width, columns), jnp.float32), offsets
    )
    return running.reshape(out_tiles * tile_width, columns)


def dense_device(
    features,
    w_self,
    w_neigh,
    layer_bias,
    tile_vals,
    tile_dst,
    tile_src,
    tile_count,
    degree,
    target_ids,
    cotangent,
):
    row_count = lax.axis_size("row")
    col_count = lax.axis_size("col")
    node_rows = features.shape[0]
    tile_width = tile_vals.shape[-1]
    cell_tiles = tile_vals[0, 0]
    cell_dst = tile_dst[0, 0]
    cell_src = tile_src[0, 0]
    usable = jnp.arange(cell_tiles.shape[0], dtype=jnp.int32) < tile_count[0, 0]
    source = lax.all_gather(features, "row", axis=0, tiled=True)
    partial_value = tile_sum(
        cell_tiles,
        cell_src,
        cell_dst,
        usable,
        source,
        col_count * node_rows // tile_width,
        False,
        0,
    )
    agg_sum = lax.psum_scatter(partial_value, "col", scatter_dimension=0, tiled=True)
    inv_degree = 1.0 / degree.astype(jnp.float32)
    aggregate = (agg_sum * inv_degree[:, None]).astype(jnp.bfloat16)
    before = (
        jnp.dot(features, w_self, preferred_element_type=jnp.float32)
        + jnp.dot(aggregate, w_neigh, preferred_element_type=jnp.float32)
        + layer_bias
    )
    hidden = gelu_value(before).astype(jnp.bfloat16)
    first_node = (lax.axis_index("row") * col_count + lax.axis_index("col")) * node_rows
    node_ids = first_node + jnp.arange(node_rows, dtype=jnp.int32)
    target = jnp.any(node_ids[:, None] == target_ids[None, :], axis=1).astype(jnp.float32)
    slope_grad = (cotangent.astype(jnp.float32) * target[:, None] * gelu_slope(before)).astype(
        jnp.bfloat16
    )
    grad_scale = 1.0 / math.sqrt(node_rows * row_count * col_count)
    contract_rows = (((0,), (0,)), ((), ()))
    self_term = lax.dot_general(
        features, slope_grad, contract_rows, preferred_element_type=jnp.float32
    )
    neigh_term = lax.dot_general(
        aggregate, slope_grad, contract_rows, preferred_element_type=jnp.float32
    )
    bias_term = jnp.sum(slope_grad.astype(jnp.float32), axis=0)
    self_sum, neigh_sum, bias_sum = lax.psum((self_term, neigh_term, bias_term), ("row", "col"))
    contract_out = (((1,), (1,)), ((), ()))
    message = (
        lax.dot_general(slope_grad, w_neigh, contract_out, preferred_element_type=jnp.float32)
        * inv_degree[:, None]
    ).astype(jnp.bfloat16)
    message_slab = lax.all_gather(message, "col", axis=0, tiled=True)
    back_part = tile_sum(
        cell_tiles,
        cell_dst,
        cell_src,
        usable,
        message_slab,
        row_count * node_rows // tile_width,
        True,
        0,
    )
    neighbour_grad = lax.psum_scatter(
        back_part.astype(jnp.bfloat16).astype(jnp.float32).astype(jnp.bfloat16),
        "row",
        scatter_dimension=0,
        tiled=True,
    ).astype(jnp.float32)
    direct = lax.dot_general(slope_grad, w_self, contract_out, preferred_element_type=jnp.float32)
    grad_features = (direct + neighbour_grad).astype(jnp.bfloat16)
    return (
        hidden,
        grad_features,
        self_sum * grad_scale,
        neigh_sum * grad_scale,
        bias_sum * grad_scale,
    )


def solution(mesh):
    in_specs = (
        P(("groups", "row", "col"), None),
        P(),
        P(),
        P(),
        P(("groups", "row"), "col", None, None, None),
        P(("groups", "row"), "col", None),
        P(("groups", "row"), "col", None),
        P(("groups", "row"), "col"),
        P(("groups", "row", "col")),
        P("groups"),
        P(("groups", "row", "col"), None),
    )
    out_specs = (
        P(("groups", "row", "col"), None),
        P(("groups", "row", "col"), None),
        P("groups", None),
        P("groups", None),
        P("groups"),
    )
    parts = mesh.shape["row"] * mesh.shape["col"]
    per_device = compact_device if parts <= 16 else dense_device
    return jax.shard_map(
        per_device, mesh=mesh, in_specs=in_specs, out_specs=out_specs, check_vma=False
    )
```

```python
import functools
import itertools
import math

import jax
import jax.numpy as jnp
from jax import lax
from jax.experimental import pallas as pl
from jax.experimental.pallas import tpu as pltpu
from jax.sharding import PartitionSpec as P

F32 = jnp.float32
BF16 = jnp.bfloat16


def gelu_value(inputs):
    return 0.5 * inputs * (1.0 + jax.scipy.special.erf(inputs * 0.7071067811865476))


def gelu_slope(inputs):
    return (
        0.5 * (1.0 + jax.scipy.special.erf(inputs * 0.7071067811865476))
        + inputs * jnp.exp(-0.5 * inputs * inputs) * 0.3989422804014327
    )


def dot(left, right, dims=((1,), (0,))):
    return lax.dot_general(left, right, (dims, ((), ())), preferred_element_type=F32)


def trade(block, axis, step):
    return lax.ppermute(block, axis, [(i, i ^ step) for i in range(lax.axis_size(axis))])


def swap_quarters(line):
    first, second, third, last = jnp.split(line, 4, axis=1)
    return jnp.concatenate([first, third, second, last], axis=1)


def flip(line, parts, bit):
    cut = jnp.split(line, parts, axis=1)
    turned = [cut[i ^ 1] for i in range(parts)]
    return jnp.where(bit == 1, jnp.concatenate(turned, axis=1), line)


def call(kernel, outputs, *inputs, spaces=(), scratch=(), out_space=pltpu.VMEM, cost=0):
    inputs = [
        pltpu.with_memory_space_constraint(x, y) if y == pltpu.HBM else x
        for x, y in itertools.zip_longest(inputs, spaces)
    ]
    spaces = list(spaces) + [pltpu.VMEM] * (len(inputs) - len(spaces))
    return pl.pallas_call(
        kernel,
        out_shape=[jax.ShapeDtypeStruct(shape, dtype) for shape, dtype in outputs],
        in_specs=[pl.BlockSpec(memory_space=space) for space in spaces],
        out_specs=[pl.BlockSpec(memory_space=out_space) for _ in outputs],
        scratch_shapes=scratch,
        cost_estimate=pl.CostEstimate(flops=int(cost * 1e9), bytes_accessed=0, transcendentals=0) if cost else None,
        compiler_params=pltpu.CompilerParams(vmem_limit_bytes=32 * 2**20),
    )(*inputs)


CFG = {'forder': [3, 1, 2], 'split': True, 'halves': [0, 1, 2, 3], 'a1': 'none', 'a2': 'found', 'dd': 'none', 'p3d': True, 'p3': [3, 1, 2], 'p3split': True, 'fp': 'found1', 'dx': 'found1', 'hid': 'none', 'cd': 3, 'fwd': False, 'ck': 0, 'cb': 0, 'cr': 0, 'cs': 0, 'cm': 0.5, 'ca': 0}


def spread(block, axis, steps):
    return {step: trade(block, axis, step) for step in steps}


def swap_bits(index):
    return index // 2 + index % 2 * 2


def select(rows, cols, ids_in, src_in, dst_in, count_in, tiles_in, cotangent_in, degree_in, *refs):
    weights_in, refs = refs[:4], refs[4:]
    adjacency, column_picks, own_picks, known, near, far, inverse, *refs = refs
    weights, (picks, src, dst, count, tiles, cotangent, degree, ids, sems) = refs[:4], refs[4:]
    pairs = [(src_in, src), (dst_in, dst), (count_in, count), (tiles_in, tiles)]
    pairs += [(cotangent_in, cotangent), (degree_in, degree), (ids_in, ids)]
    pairs += list(zip(weights_in, weights))
    copies = [pltpu.make_async_copy(a, b, sems.at[i]) for i, (a, b) in enumerate(pairs)]
    for copy in copies:
        copy.start()
    row, col = lax.axis_index("row"), lax.axis_index("col")
    slots, (nodes, width) = ids.shape[1], cotangent.shape
    adjacency[...] = jnp.zeros(adjacency.shape, adjacency.dtype)
    for copy in copies[:7]:
        copy.wait()
    for k in range(tiles.shape[2]):

        @pl.when(k < count[0, 0])
        def _():
            down = pl.multiple_of(swap_bits(dst[0, 0, k] ^ col) * nodes, nodes)
            adjacency[src[0, 0, k] ^ row, pl.ds(down, nodes), :] = tiles[0, 0, k]

    line = flip(flip(swap_quarters(ids[...]), 2, col % 2), 4, col // 2)
    line = jnp.broadcast_to(line, (nodes, slots))
    stack = line.T
    lanes = lax.broadcasted_iota(jnp.int32, (slots, nodes), 1)
    for k in range(cols):
        base = (row * cols + (col ^ swap_bits(k))) * nodes
        picks[:, k * nodes : (k + 1) * nodes] = (stack == lanes + base).astype(BF16)
    for s in range(rows):
        base = ((row ^ s) * cols + col) * nodes
        column_picks[:, s * nodes : (s + 1) * nodes] = (stack == lanes + base).astype(BF16)
    base = (row * cols + col) * nodes
    across = lax.broadcasted_iota(jnp.int32, (nodes, slots), 0)
    own_picks[...] = (line == across + base).astype(BF16)
    for s in range(rows):
        block = dot(picks[...], adjacency[s]).astype(BF16)
        index = list(CFG["halves"]).index(s)
        (far if index // 2 else near)[index % 2 * slots : (index % 2 + 1) * slots, :] = block
    own = picks[:, :nodes]
    known[:, :width] = dot(own, cotangent[...]).astype(BF16)
    for copy in copies[7:]:
        copy.wait()
    counts = degree[...].astype(F32)
    inverse[...] = 1.0 / jnp.broadcast_to(counts, (nodes, nodes)).T
    counts = jnp.sum(own.astype(F32) * counts, axis=1, keepdims=True)
    known[:, width:] = jnp.broadcast_to(counts, (slots, 128)).astype(BF16)


def block_of(step, near, far, slots):
    index = list(CFG["halves"]).index(step)
    return (far if index // 2 else near)[index % 2 * slots : (index % 2 + 1) * slots, :]


def dense_part(steps, adjacency, *refs):
    *features, kept, sent = refs
    total = sum(dot(adjacency[step], block[...]) for step, block in zip(steps, features))
    half = kept.shape[0]
    kept[...] = total[:half]
    sent[...] = total[half:].astype(BF16)


def begin(step, column_picks, features, near, far, total, chosen):
    slots, nodes = column_picks.shape[0], features.shape[0]
    total[...] = dot(block_of(step, near, far, slots), features[...])
    chosen[...] = dot(column_picks[:, step * nodes : (step + 1) * nodes], features[...])


def combine(steps, column_picks, known, *refs):
    features, (near, far, *first, sent, part, fixed) = refs[: len(steps)], refs[len(steps) :]
    nodes, width = features[0].shape
    half = part.shape[0]
    sums, picked = [x[...] for x in first] or [0.0, 0.0]
    for step, block in zip(steps, features):
        sums += dot(block_of(step, near, far, 2 * half), block[...])
        picked += dot(column_picks[:, step * nodes : (step + 1) * nodes], block[...])
    picked = picked.astype(BF16)
    part[...] = sums[:half]
    fixed[:, :width] = picked[:half]
    fixed[:, width:] = known[:half, :]
    sent[:, :width] = sums[half:].astype(BF16)
    sent[:, width : 2 * width] = picked[half:]
    sent[:, 2 * width :] = known[half:, :]


def relay(part, fixed, got, sent, part_out, fixed_out):
    share, width = part_out.shape
    sums = part[...] + got[:, :width].astype(F32)
    rest = fixed[...] + got[:, width:]
    part_out[...] = sums[:share]
    fixed_out[...] = rest[:share]
    sent[:, :width] = sums[share:].astype(BF16)
    sent[:, width:] = rest[share:]


def slopes(part, fixed, got, w_self, w_neigh, layer_bias, found, features):
    width = part.shape[1]
    total = part[...] + got[:, :width].astype(F32)
    rest = fixed[...] + got[:, width:]
    features[...] = rest[:, :width]
    cotangent = rest[:, width : 2 * width].astype(F32)
    degrees = rest[:, 2 * width :]
    degree = degrees[:, :1].astype(F32)
    inverse = jnp.where(degree > 0, 1.0 / jnp.maximum(degree, 1.0), 0.0)
    aggregate = (total * inverse).astype(BF16)
    before = dot(rest[:, :width], w_self[...]) + dot(aggregate, w_neigh[...]) + layer_bias[...]
    slope = (cotangent * gelu_slope(before)).astype(BF16)
    share, bands = part.shape[0], width // 128
    for b in range(bands):
        found[b * share : (b + 1) * share, :] = slope[:, b * 128 : (b + 1) * 128]
        down = (bands + b) * share
        found[down : down + share, :] = aggregate[:, b * 128 : (b + 1) * 128]
    line = degrees.astype(F32).T[:16, :]
    line = jnp.concatenate([line, jnp.zeros((16, 128 - share), F32)], axis=1)
    found[2 * bands * share :, :] = line.astype(BF16)


def merge(*refs):
    refs[-1][...] = sum(part[...] for part in refs[:-1])


def activate(features, total, got, inverse, w_self, w_neigh, layer_bias, hidden):
    total = total[...] + got[...].astype(F32)
    aggregate = (total * inverse[:, :1]).astype(BF16)
    before = dot(features[...], w_self[...]) + dot(aggregate, w_neigh[...]) + layer_bias[...]
    hidden[...] = gelu_value(before).astype(BF16)


def finish(scale, *refs):
    found, features, refs = refs[:2], refs[2:4], refs[4:]
    own_columns, own_picks, w_self, w_neigh, *refs = refs
    outs, (slope, aggregate, *results, sems) = refs[:4], refs[4:]
    grad_features, grad_self, grad_neigh, grad_bias = results
    slots, width = slope.shape
    half, bands = slots // 2, width // 128
    share = half // 2
    size = found[0].shape[0] // 2
    front, back = ((0,), (0,)), ((1,), (1,))
    degrees = []
    for q in range(4):
        part, base, here = found[q // 2], q % 2 * size, slice(q * share, (q + 1) * share)
        for b in range(bands):
            lanes = slice(b * 128, (b + 1) * 128)
            slope[here, lanes] = part[base + b * share : base + (b + 1) * share, :]
            down = base + (bands + b) * share
            aggregate[here, lanes] = part[down : down + share, :]
        degrees.append(part[base + size - 16 : base + size, :].astype(F32)[:1, :share])
    copies = [pltpu.make_async_copy(a, b, sems.at[i]) for i, (a, b) in enumerate(zip(results, outs))]
    grad_self[...] = scale * (
        dot(features[0][...], slope[:half, :], front)
        + dot(features[1][...], slope[half:, :], front)
    )
    copies[1].start()
    grad_neigh[...] = dot(aggregate[...], slope[...], front) * scale
    copies[2].start()
    grad_bias[...] = jnp.sum(slope[...].astype(F32), axis=0, keepdims=True) * scale
    copies[3].start()
    degree = jnp.broadcast_to(jnp.concatenate(degrees, axis=1), (128, slots)).T[:, :1]
    message = (dot(slope[...], w_neigh[...], back) / degree).astype(BF16)
    own_slope = dot(own_picks[...], slope[...]).astype(BF16)
    total = dot(own_slope, w_self[...], back) + dot(own_columns[...], message, front)
    grad_features[...] = total.astype(BF16)
    copies[0].start()
    for copy in copies:
        copy.wait()


def compact_device(
    features,
    w_self,
    w_neigh,
    layer_bias,
    tile_vals,
    tile_dst,
    tile_src,
    tile_count,
    degree,
    target_ids,
    cotangent,
):
    rows = lax.axis_size("row")
    cols = lax.axis_size("col")
    nodes, width = features.shape
    slots = target_ids.shape[0]
    share = slots // cols
    half = slots // 2

    tie = lax.optimization_barrier
    if CFG["fwd"]:
        feature_parts = spread(features, "row", (2, 1))
        feature_parts[3] = trade(feature_parts[2], "row", 1)
    else:
        feature_parts = spread(features, "row", tuple(CFG["forder"]))
    steps = tuple(CFG["forder"])
    raw_features = features

    bias = layer_bias.reshape(1, width)
    adjacency, column_picks, own_picks, known, near, far, inverse, *resident = call(
        functools.partial(select, rows, cols),
        [
            ((rows, cols * nodes, nodes), BF16),
            ((slots, rows * nodes), BF16),
            ((nodes, slots), BF16),
            ((slots, width + 128), BF16),
        ]
        + [((rows // 2 * slots, nodes), BF16)] * 2
        + [((nodes, nodes), F32)]
        + [((width, width), BF16)] * 2
        + [((1, width), F32), ((nodes, width), BF16)],
        target_ids.reshape(1, slots),
        tile_src,
        tile_dst,
        tile_count,
        tile_vals,
        cotangent,
        degree.reshape(1, nodes),
        w_self,
        w_neigh,
        bias,
        raw_features,
        spaces=[pltpu.HBM] * 3 + [pl.ANY] + [pltpu.HBM] * 7,
        cost=CFG["ck"],
        scratch=[pltpu.VMEM((slots, cols * nodes), BF16)]
        + [pltpu.SMEM(x.shape, x.dtype) for x in (tile_src, tile_dst, tile_count)]
        + [pltpu.VMEM(x.shape, x.dtype) for x in (tile_vals, cotangent)]
        + [pltpu.VMEM((1, nodes), jnp.int32), pltpu.VMEM((1, slots), jnp.int32)]
        + [pltpu.SemaphoreType.DMA((11,))],
    )
    w_self, w_neigh, bias, features = resident
    feature_parts[0] = features
    first = ()
    if CFG["split"]:
        first = call(
            functools.partial(begin, steps[0]),
            [((slots, width), F32)] * 2,
            column_picks,
            feature_parts[steps[0]],
            near,
            far,
            cost=CFG["cb"],
        )
    later = steps[len(first) // 2 :] + (0,)
    sent, part, fixed = call(
        functools.partial(combine, later),
        [((half, 3 * width + 128), BF16), ((half, width), F32), ((half, 2 * width + 128), BF16)],
        column_picks,
        known,
        *[feature_parts[step] for step in later],
        near,
        far,
        *first,
        cost=CFG["cb"],
    )
    got = trade(sent, "col", 1)
    sent, part, fixed = call(
        relay,
        [((share, 3 * width + 128), BF16), ((share, width), F32), ((share, 2 * width + 128), BF16)],
        part,
        fixed,
        got,
        cost=CFG["cr"],
    )
    if CFG["a1"] == "sent":
        sent, far = tie((sent, far))
    if CFG["dd"] == "sent":
        sent, feature_parts = tie((sent, feature_parts))
    got = trade(sent, "col", 2)
    found, feature_slots = call(
        slopes,
        [((2 * (width // 128) * share + 16, 128), BF16), ((share, width), BF16)],
        part,
        fixed,
        got,
        w_self,
        w_neigh,
        bias,
        cost=CFG["cs"],
    )
    if CFG["a1"] == "found":
        found, far = tie((found, far))
    if CFG["dd"] == "found":
        found, feature_parts = tie((found, feature_parts))
    near_step, far_step = CFG["halves"][1], CFG["halves"][2]
    columns = near + trade(far, "row", far_step)
    if CFG["a2"] == "found":
        found, columns = tie((found, columns))

    def prepare_dense(feature_parts):
        kept, dense = call(
            functools.partial(dense_part, steps + (0,)),
            [((2 * nodes, width), F32), ((2 * nodes, width), BF16)],
            adjacency,
            *[feature_parts[step] for step in steps + (0,)],
            cost=CFG["cd"],
        )
        return kept + trade(dense, "col", 1).astype(F32)

    dense = prepare_dense(feature_parts)
    parts = spread(found, "row", CFG["p3"]) if CFG["p3d"] else None
    if CFG["p3d"]:
        if CFG["p3split"]:
            (found,) = call(merge, [(found.shape, BF16)], *[parts.pop(CFG["p3"][0]), found], cost=CFG["cm"])
    else:
        (found,) = call(merge, [(found.shape, BF16)], *[trade(found, "row", CFG["p3"][0]), found], cost=CFG["cm"])
    if CFG["a2"] == "found1":
        found, columns = tie((found, columns))
    if CFG["fp"] == "found1":
        found, feature_slots = tie((found, feature_slots))
    if CFG["dx"] == "found1":
        found, dense = tie((found, dense))
    if CFG["p3d"]:
        (found,) = call(merge, [(found.shape, BF16)], *[*parts.values(), found], cost=CFG["cm"])
    else:
        (found,) = call(merge, [(found.shape, BF16)], *[trade(found, "row", CFG["p3"][1]), found], cost=CFG["cm"])
    if CFG["dx"] == "merged":
        found, dense = tie((found, dense))
    own_columns = columns[:slots] + trade(columns[slots:], "row", near_step)
    if CFG["fp"] == "join":
        joined = jnp.concatenate([feature_slots, dense[nodes:].astype(BF16)], axis=0)
        found, joined = tie((found, joined))
        joined = trade(joined, "col", 2)
        feature_mine = jnp.concatenate([feature_slots, joined[:share]], axis=0)
        dense_got = joined[share:]
    else:
        dense_got = trade(dense[nodes:].astype(BF16), "col", 2)
        feature_mine = jnp.concatenate([feature_slots, trade(feature_slots, "col", 2)], axis=0)
    if CFG["fp"] != "none":
        feature_other = trade(feature_mine, "col", 1)
        everything = found
    else:
        everything = jnp.concatenate([found, feature_slots], axis=1)
    found_mine = jnp.concatenate([everything, trade(everything, "col", 2)], axis=0)
    if CFG["hid"] == "mine":
        found_mine, dense_got = tie((found_mine, dense_got))
    found_other = trade(found_mine, "col", 1)
    if CFG["fp"] == "none":
        feature_mine, feature_other = found_mine[:, -width:], found_other[:, -width:]
    (hidden,) = call(
        activate,
        [((nodes, width), BF16)],
        features,
        dense[:nodes],
        dense_got,
        inverse,
        w_self,
        w_neigh,
        bias,
        cost=CFG["ca"],
    )
    results = [((nodes, width), BF16), ((width, width), F32), ((width, width), F32), ((1, width), F32)]
    grad_features, grad_self, grad_neigh, grad_bias = call(
        functools.partial(finish, 1.0 / math.sqrt(nodes * rows * cols)),
        results,
        found_mine,
        found_other,
        feature_mine,
        feature_other,
        own_columns,
        own_picks,
        w_self,
        w_neigh,
        scratch=[pltpu.VMEM((slots, width), BF16)] * 2
        + [pltpu.VMEM(*result) for result in results]
        + [pltpu.SemaphoreType.DMA((4,))],
        out_space=pl.ANY,
    )
    return (hidden, grad_features, grad_self, grad_neigh, grad_bias.reshape(width))


def tile_sum(values, take_index, put_index, usable, source, out_tiles, transpose, first_tile):
    slot_count, tile_width = (values.shape[0], values.shape[1])
    columns = source.shape[1]
    blocks = source.reshape(-1, tile_width, columns)
    group_size = math.gcd(slot_count, 16)
    pattern = "kji,kjf->kif" if transpose else "kij,kjf->kif"

    def advance(running, offset):
        tile_block = lax.dynamic_slice_in_dim(values, offset, group_size, 0)
        taken = lax.dynamic_slice_in_dim(take_index, offset, group_size, 0)
        placed = lax.dynamic_slice_in_dim(put_index, offset, group_size, 0) - first_tile
        allowed = lax.dynamic_slice_in_dim(usable, offset, group_size, 0)
        inside = allowed & (placed >= 0) & (placed < out_tiles)
        chosen = blocks[taken]
        product = jnp.einsum(pattern, tile_block, chosen, preferred_element_type=jnp.float32)
        product = product * inside.astype(jnp.float32)[:, None, None]
        where_to = jnp.where(inside, placed, 0)
        running = running.at[where_to].add(product)
        return (running, None)

    offsets = jnp.arange(0, slot_count, group_size, dtype=jnp.int32)
    running, _ = lax.scan(
        advance, jnp.zeros((out_tiles, tile_width, columns), jnp.float32), offsets
    )
    return running.reshape(out_tiles * tile_width, columns)


def dense_device(
    features,
    w_self,
    w_neigh,
    layer_bias,
    tile_vals,
    tile_dst,
    tile_src,
    tile_count,
    degree,
    target_ids,
    cotangent,
):
    row_count = lax.axis_size("row")
    col_count = lax.axis_size("col")
    node_rows = features.shape[0]
    tile_width = tile_vals.shape[-1]
    cell_tiles = tile_vals[0, 0]
    cell_dst = tile_dst[0, 0]
    cell_src = tile_src[0, 0]
    usable = jnp.arange(cell_tiles.shape[0], dtype=jnp.int32) < tile_count[0, 0]
    source = lax.all_gather(features, "row", axis=0, tiled=True)
    partial_value = tile_sum(
        cell_tiles,
        cell_src,
        cell_dst,
        usable,
        source,
        col_count * node_rows // tile_width,
        False,
        0,
    )
    agg_sum = lax.psum_scatter(partial_value, "col", scatter_dimension=0, tiled=True)
    inv_degree = 1.0 / degree.astype(jnp.float32)
    aggregate = (agg_sum * inv_degree[:, None]).astype(jnp.bfloat16)
    before = (
        jnp.dot(features, w_self, preferred_element_type=jnp.float32)
        + jnp.dot(aggregate, w_neigh, preferred_element_type=jnp.float32)
        + layer_bias
    )
    hidden = gelu_value(before).astype(jnp.bfloat16)
    first_node = (lax.axis_index("row") * col_count + lax.axis_index("col")) * node_rows
    node_ids = first_node + jnp.arange(node_rows, dtype=jnp.int32)
    target = jnp.any(node_ids[:, None] == target_ids[None, :], axis=1).astype(jnp.float32)
    slope_grad = (cotangent.astype(jnp.float32) * target[:, None] * gelu_slope(before)).astype(
        jnp.bfloat16
    )
    grad_scale = 1.0 / math.sqrt(node_rows * row_count * col_count)
    contract_rows = (((0,), (0,)), ((), ()))
    self_term = lax.dot_general(
        features, slope_grad, contract_rows, preferred_element_type=jnp.float32
    )
    neigh_term = lax.dot_general(
        aggregate, slope_grad, contract_rows, preferred_element_type=jnp.float32
    )
    bias_term = jnp.sum(slope_grad.astype(jnp.float32), axis=0)
    self_sum, neigh_sum, bias_sum = lax.psum((self_term, neigh_term, bias_term), ("row", "col"))
    contract_out = (((1,), (1,)), ((), ()))
    message = (
        lax.dot_general(slope_grad, w_neigh, contract_out, preferred_element_type=jnp.float32)
        * inv_degree[:, None]
    ).astype(jnp.bfloat16)
    message_slab = lax.all_gather(message, "col", axis=0, tiled=True)
    back_part = tile_sum(
        cell_tiles,
        cell_dst,
        cell_src,
        usable,
        message_slab,
        row_count * node_rows // tile_width,
        True,
        0,
    )
    neighbour_grad = lax.psum_scatter(
        back_part.astype(jnp.bfloat16).astype(jnp.float32).astype(jnp.bfloat16),
        "row",
        scatter_dimension=0,
        tiled=True,
    ).astype(jnp.float32)
    direct = lax.dot_general(slope_grad, w_self, contract_out, preferred_element_type=jnp.float32)
    grad_features = (direct + neighbour_grad).astype(jnp.bfloat16)
    return (
        hidden,
        grad_features,
        self_sum * grad_scale,
        neigh_sum * grad_scale,
        bias_sum * grad_scale,
    )


def solution(mesh):
    in_specs = (
        P(("groups", "row", "col"), None),
        P(),
        P(),
        P(),
        P(("groups", "row"), "col", None, None, None),
        P(("groups", "row"), "col", None),
        P(("groups", "row"), "col", None),
        P(("groups", "row"), "col"),
        P(("groups", "row", "col")),
        P("groups"),
        P(("groups", "row", "col"), None),
    )
    out_specs = (
        P(("groups", "row", "col"), None),
        P(("groups", "row", "col"), None),
        P("groups", None),
        P("groups", None),
        P("groups"),
    )
    parts = mesh.shape["row"] * mesh.shape["col"]
    per_device = compact_device if parts <= 16 else dense_device
    return jax.shard_map(
        per_device, mesh=mesh, in_specs=in_specs, out_specs=out_specs, check_vma=False
    )
```

```python
import functools
import itertools
import math

import jax
import jax.numpy as jnp
from jax import lax
from jax.experimental import pallas as pl
from jax.experimental.pallas import tpu as pltpu
from jax.sharding import PartitionSpec as P

F32 = jnp.float32
BF16 = jnp.bfloat16


def gelu_value(inputs):
    return 0.5 * inputs * (1.0 + jax.scipy.special.erf(inputs * 0.7071067811865476))


def gelu_slope(inputs):
    return (
        0.5 * (1.0 + jax.scipy.special.erf(inputs * 0.7071067811865476))
        + inputs * jnp.exp(-0.5 * inputs * inputs) * 0.3989422804014327
    )


def dot(left, right, dims=((1,), (0,))):
    return lax.dot_general(left, right, (dims, ((), ())), preferred_element_type=F32)


def trade(block, axis, step):
    return lax.ppermute(block, axis, [(i, i ^ step) for i in range(lax.axis_size(axis))])


def swap_quarters(line):
    first, second, third, last = jnp.split(line, 4, axis=1)
    return jnp.concatenate([first, third, second, last], axis=1)


def flip(line, parts, bit):
    cut = jnp.split(line, parts, axis=1)
    turned = [cut[i ^ 1] for i in range(parts)]
    return jnp.where(bit == 1, jnp.concatenate(turned, axis=1), line)


MERGE_COST = pl.CostEstimate(flops=2 * 10**9, bytes_accessed=0, transcendentals=0)
DENSE_COST = pl.CostEstimate(flops=3 * 10**9, bytes_accessed=0, transcendentals=0)


def call(kernel, outputs, *inputs, spaces=(), scratch=(), out_space=pltpu.VMEM, cost=None):
    inputs = [
        pltpu.with_memory_space_constraint(x, y) if y == pltpu.HBM else x
        for x, y in itertools.zip_longest(inputs, spaces)
    ]
    spaces = list(spaces) + [pltpu.VMEM] * (len(inputs) - len(spaces))
    return pl.pallas_call(
        kernel,
        out_shape=[jax.ShapeDtypeStruct(shape, dtype) for shape, dtype in outputs],
        in_specs=[pl.BlockSpec(memory_space=space) for space in spaces],
        out_specs=[pl.BlockSpec(memory_space=out_space) for _ in outputs],
        scratch_shapes=scratch,
        cost_estimate=cost,
        compiler_params=pltpu.CompilerParams(vmem_limit_bytes=32 * 2**20),
    )(*inputs)


def spread(block, axis, steps):
    return {step: trade(block, axis, step) for step in steps}


def swap_bits(index):
    return index // 2 + index % 2 * 2


def select(rows, cols, ids_in, src_in, dst_in, count_in, tiles_in, cotangent_in, degree_in, *refs):
    weights_in, refs = refs[:4], refs[4:]
    adjacency, column_picks, own_picks, known, near, far, inverse, *refs = refs
    weights, (picks, src, dst, count, tiles, cotangent, degree, ids, sems) = refs[:4], refs[4:]
    pairs = [(ids_in, ids), (cotangent_in, cotangent), (degree_in, degree), (tiles_in, tiles)]
    pairs += [(src_in, src), (dst_in, dst), (count_in, count)]
    pairs += list(zip(weights_in, weights))
    copies = [pltpu.make_async_copy(a, b, sems.at[i]) for i, (a, b) in enumerate(pairs)]
    for copy in copies:
        copy.start()
    row, col = lax.axis_index("row"), lax.axis_index("col")
    slots, (nodes, width) = ids.shape[1], cotangent.shape
    adjacency[...] = jnp.zeros(adjacency.shape, adjacency.dtype)
    copies[0].wait()
    line = flip(flip(swap_quarters(ids[...]), 2, col % 2), 4, col // 2)
    line = jnp.broadcast_to(line, (nodes, slots))
    stack = line.T
    lanes = lax.broadcasted_iota(jnp.int32, (slots, nodes), 1)
    for k in range(cols):
        base = (row * cols + (col ^ swap_bits(k))) * nodes
        picks[:, k * nodes : (k + 1) * nodes] = (stack == lanes + base).astype(BF16)
    for s in range(rows):
        base = ((row ^ s) * cols + col) * nodes
        column_picks[:, s * nodes : (s + 1) * nodes] = (stack == lanes + base).astype(BF16)
    base = (row * cols + col) * nodes
    across = lax.broadcasted_iota(jnp.int32, (nodes, slots), 0)
    own_picks[...] = (line == across + base).astype(BF16)
    for copy in copies[1:3]:
        copy.wait()
    own = picks[:, :nodes]
    known[:, :width] = dot(own, cotangent[...]).astype(BF16)
    counts = degree[...].astype(F32)
    inverse[...] = 1.0 / jnp.broadcast_to(counts, (nodes, nodes)).T
    counts = jnp.sum(own.astype(F32) * counts, axis=1, keepdims=True)
    known[:, width:] = jnp.broadcast_to(counts, (slots, 128)).astype(BF16)
    for copy in copies[3:]:
        copy.wait()
    for k in range(tiles.shape[2]):

        @pl.when(k < count[0, 0])
        def _():
            down = pl.multiple_of(swap_bits(dst[0, 0, k] ^ col) * nodes, nodes)
            adjacency[src[0, 0, k] ^ row, pl.ds(down, nodes), :] = tiles[0, 0, k]

    for s in range(rows):
        block = dot(picks[...], adjacency[s]).astype(BF16)
        (far if s // 2 else near)[s % 2 * slots : (s % 2 + 1) * slots, :] = block


def block_of(step, near, far, slots):
    return (far if step // 2 else near)[step % 2 * slots : (step % 2 + 1) * slots, :]


def dense_part(steps, adjacency, *refs):
    *features, kept, sent = refs
    total = sum(dot(adjacency[step], block[...]) for step, block in zip(steps, features))
    half = kept.shape[0]
    kept[...] = total[:half]
    sent[...] = total[half:].astype(BF16)


def combine(steps, column_picks, known, *refs):
    features, (near, far, sent, part, fixed) = refs[: len(steps)], refs[len(steps) :]
    nodes, width = features[0].shape
    half = part.shape[0]
    sums, picked = 0.0, 0.0
    for step, block in zip(steps, features):
        sums += dot(block_of(step, near, far, 2 * half), block[...])
        picked += dot(column_picks[:, step * nodes : (step + 1) * nodes], block[...])
    picked = picked.astype(BF16)
    part[...] = sums[:half]
    fixed[:, :width] = picked[:half]
    fixed[:, width:] = known[:half, :]
    sent[:, :width] = sums[half:].astype(BF16)
    sent[:, width : 2 * width] = picked[half:]
    sent[:, 2 * width :] = known[half:, :]


def relay(part, fixed, got, sent, part_out, fixed_out):
    share, width = part_out.shape
    sums = part[...] + got[:, :width].astype(F32)
    rest = fixed[...] + got[:, width:]
    part_out[...] = sums[:share]
    fixed_out[...] = rest[:share]
    sent[:, :width] = sums[share:].astype(BF16)
    sent[:, width:] = rest[share:]


def slopes(part, fixed, got, w_self, w_neigh, layer_bias, found, features):
    width = part.shape[1]
    total = part[...] + got[:, :width].astype(F32)
    rest = fixed[...] + got[:, width:]
    features[...] = rest[:, :width]
    cotangent = rest[:, width : 2 * width].astype(F32)
    degrees = rest[:, 2 * width :]
    degree = degrees[:, :1].astype(F32)
    inverse = jnp.where(degree > 0, 1.0 / jnp.maximum(degree, 1.0), 0.0)
    aggregate = (total * inverse).astype(BF16)
    before = dot(rest[:, :width], w_self[...]) + dot(aggregate, w_neigh[...]) + layer_bias[...]
    slope = (cotangent * gelu_slope(before)).astype(BF16)
    share, bands = part.shape[0], width // 128
    for b in range(bands):
        found[b * share : (b + 1) * share, :] = slope[:, b * 128 : (b + 1) * 128]
        down = (bands + b) * share
        found[down : down + share, :] = aggregate[:, b * 128 : (b + 1) * 128]
    line = degrees.astype(F32).T[:16, :]
    line = jnp.concatenate([line, jnp.zeros((16, 128 - share), F32)], axis=1)
    found[2 * bands * share :, :] = line.astype(BF16)


def merge(*refs):
    refs[-1][...] = sum(part[...] for part in refs[:-1])


def activate(features, total, got, inverse, w_self, w_neigh, layer_bias, hidden):
    total = total[...] + got[...].astype(F32)
    aggregate = (total * inverse[:, :1]).astype(BF16)
    before = dot(features[...], w_self[...]) + dot(aggregate, w_neigh[...]) + layer_bias[...]
    hidden[...] = gelu_value(before).astype(BF16)


def finish(scale, *refs):
    found, features, refs = refs[:2], refs[2:4], refs[4:]
    own_columns, own_picks, w_self, w_neigh, *refs = refs
    outs, (slope, aggregate, *results, sems) = refs[:4], refs[4:]
    grad_features, grad_self, grad_neigh, grad_bias = results
    slots, width = slope.shape
    half, bands = slots // 2, width // 128
    share = half // 2
    size = found[0].shape[0] // 2
    front, back = ((0,), (0,)), ((1,), (1,))
    degrees = []
    for q in range(4):
        part, base, here = found[q // 2], q % 2 * size, slice(q * share, (q + 1) * share)
        for b in range(bands):
            lanes = slice(b * 128, (b + 1) * 128)
            slope[here, lanes] = part[base + b * share : base + (b + 1) * share, :]
            down = base + (bands + b) * share
            aggregate[here, lanes] = part[down : down + share, :]
        degrees.append(part[base + size - 16 : base + size, :].astype(F32)[:1, :share])
    copies = [pltpu.make_async_copy(a, b, sems.at[i]) for i, (a, b) in enumerate(zip(results, outs))]
    grad_self[...] = scale * (
        dot(features[0][...], slope[:half, :], front)
        + dot(features[1][...], slope[half:, :], front)
    )
    copies[1].start()
    grad_neigh[...] = dot(aggregate[...], slope[...], front) * scale
    copies[2].start()
    grad_bias[...] = jnp.sum(slope[...].astype(F32), axis=0, keepdims=True) * scale
    copies[3].start()
    degree = jnp.broadcast_to(jnp.concatenate(degrees, axis=1), (128, slots)).T[:, :1]
    message = (dot(slope[...], w_neigh[...], back) / degree).astype(BF16)
    own_slope = dot(own_picks[...], slope[...]).astype(BF16)
    total = dot(own_slope, w_self[...], back) + dot(own_columns[...], message, front)
    grad_features[...] = total.astype(BF16)
    copies[0].start()
    for copy in copies:
        copy.wait()


def compact_device(
    features,
    w_self,
    w_neigh,
    layer_bias,
    tile_vals,
    tile_dst,
    tile_src,
    tile_count,
    degree,
    target_ids,
    cotangent,
):
    rows = lax.axis_size("row")
    cols = lax.axis_size("col")
    nodes, width = features.shape
    slots = target_ids.shape[0]
    share = slots // cols
    half = slots // 2

    order = (3, 1, 2)
    feature_parts = spread(features, "row", order)

    bias = layer_bias.reshape(1, width)
    adjacency, column_picks, own_picks, known, near, far, inverse, *resident = call(
        functools.partial(select, rows, cols),
        [
            ((rows, cols * nodes, nodes), BF16),
            ((slots, rows * nodes), BF16),
            ((nodes, slots), BF16),
            ((slots, width + 128), BF16),
        ]
        + [((rows // 2 * slots, nodes), BF16)] * 2
        + [((nodes, nodes), F32)]
        + [((width, width), BF16)] * 2
        + [((1, width), F32), ((nodes, width), BF16)],
        target_ids.reshape(1, slots),
        tile_src,
        tile_dst,
        tile_count,
        tile_vals,
        cotangent,
        degree.reshape(1, nodes),
        w_self,
        w_neigh,
        bias,
        features,
        spaces=[pltpu.HBM] * 3 + [pl.ANY] + [pltpu.HBM] * 7,
        scratch=[pltpu.VMEM((slots, cols * nodes), BF16)]
        + [pltpu.SMEM(x.shape, x.dtype) for x in (tile_src, tile_dst, tile_count)]
        + [pltpu.VMEM(x.shape, x.dtype) for x in (tile_vals, cotangent)]
        + [pltpu.VMEM((1, nodes), jnp.int32), pltpu.VMEM((1, slots), jnp.int32)]
        + [pltpu.SemaphoreType.DMA((11,))],
    )
    w_self, w_neigh, bias, features = resident
    feature_parts[0] = features
    sent, part, fixed = call(
        functools.partial(combine, order + (0,)),
        [((half, 3 * width + 128), BF16), ((half, width), F32), ((half, 2 * width + 128), BF16)],
        column_picks,
        known,
        *[feature_parts[step] for step in order + (0,)],
        near,
        far,
    )
    got = trade(sent, "col", 1)
    sent, part, fixed = call(
        relay,
        [((share, 3 * width + 128), BF16), ((share, width), F32), ((share, 2 * width + 128), BF16)],
        part,
        fixed,
        got,
    )
    got = trade(sent, "col", 2)
    found, feature_slots = call(
        slopes,
        [((2 * (width // 128) * share + 16, 128), BF16), ((share, width), BF16)],
        part,
        fixed,
        got,
        w_self,
        w_neigh,
        bias,
    )
    columns = near + trade(far, "row", 2)
    found, columns = lax.optimization_barrier((found, columns))
    dense, dense_sent = call(
        functools.partial(dense_part, order + (0,)),
        [((2 * nodes, width), F32), ((2 * nodes, width), BF16)],
        adjacency,
        *[feature_parts[step] for step in order + (0,)],
        cost=DENSE_COST,
    )
    dense = dense + trade(dense_sent, "col", 1).astype(F32)
    parts = spread(found, "row", order)
    (found,) = call(merge, [(found.shape, BF16)], parts.pop(order[0]), found, cost=MERGE_COST)
    found, feature_slots = lax.optimization_barrier((found, feature_slots))
    found, dense = lax.optimization_barrier((found, dense))
    (found,) = call(merge, [(found.shape, BF16)], *parts.values(), found, cost=MERGE_COST)
    own_columns = columns[:slots] + trade(columns[slots:], "row", 1)
    dense_got = trade(dense[nodes:].astype(BF16), "col", 2)
    feature_mine = jnp.concatenate([feature_slots, trade(feature_slots, "col", 2)], axis=0)
    feature_other = trade(feature_mine, "col", 1)
    found_mine = jnp.concatenate([found, trade(found, "col", 2)], axis=0)
    found_other = trade(found_mine, "col", 1)
    (hidden,) = call(
        activate,
        [((nodes, width), BF16)],
        features,
        dense[:nodes],
        dense_got,
        inverse,
        w_self,
        w_neigh,
        bias,
    )
    results = [((nodes, width), BF16), ((width, width), F32), ((width, width), F32), ((1, width), F32)]
    grad_features, grad_self, grad_neigh, grad_bias = call(
        functools.partial(finish, 1.0 / math.sqrt(nodes * rows * cols)),
        results,
        found_mine,
        found_other,
        feature_mine,
        feature_other,
        own_columns,
        own_picks,
        w_self,
        w_neigh,
        scratch=[pltpu.VMEM((slots, width), BF16)] * 2
        + [pltpu.VMEM(*result) for result in results]
        + [pltpu.SemaphoreType.DMA((4,))],
        out_space=pl.ANY,
    )
    return (hidden, grad_features, grad_self, grad_neigh, grad_bias.reshape(width))


def tile_sum(values, take_index, put_index, usable, source, out_tiles, transpose, first_tile):
    slot_count, tile_width = (values.shape[0], values.shape[1])
    columns = source.shape[1]
    blocks = source.reshape(-1, tile_width, columns)
    group_size = math.gcd(slot_count, 16)
    pattern = "kji,kjf->kif" if transpose else "kij,kjf->kif"

    def advance(running, offset):
        tile_block = lax.dynamic_slice_in_dim(values, offset, group_size, 0)
        taken = lax.dynamic_slice_in_dim(take_index, offset, group_size, 0)
        placed = lax.dynamic_slice_in_dim(put_index, offset, group_size, 0) - first_tile
        allowed = lax.dynamic_slice_in_dim(usable, offset, group_size, 0)
        inside = allowed & (placed >= 0) & (placed < out_tiles)
        chosen = blocks[taken]
        product = jnp.einsum(pattern, tile_block, chosen, preferred_element_type=jnp.float32)
        product = product * inside.astype(jnp.float32)[:, None, None]
        where_to = jnp.where(inside, placed, 0)
        running = running.at[where_to].add(product)
        return (running, None)

    offsets = jnp.arange(0, slot_count, group_size, dtype=jnp.int32)
    running, _ = lax.scan(
        advance, jnp.zeros((out_tiles, tile_width, columns), jnp.float32), offsets
    )
    return running.reshape(out_tiles * tile_width, columns)


def dense_device(
    features,
    w_self,
    w_neigh,
    layer_bias,
    tile_vals,
    tile_dst,
    tile_src,
    tile_count,
    degree,
    target_ids,
    cotangent,
):
    row_count = lax.axis_size("row")
    col_count = lax.axis_size("col")
    node_rows = features.shape[0]
    tile_width = tile_vals.shape[-1]
    cell_tiles = tile_vals[0, 0]
    cell_dst = tile_dst[0, 0]
    cell_src = tile_src[0, 0]
    usable = jnp.arange(cell_tiles.shape[0], dtype=jnp.int32) < tile_count[0, 0]
    source = lax.all_gather(features, "row", axis=0, tiled=True)
    partial_value = tile_sum(
        cell_tiles,
        cell_src,
        cell_dst,
        usable,
        source,
        col_count * node_rows // tile_width,
        False,
        0,
    )
    agg_sum = lax.psum_scatter(partial_value, "col", scatter_dimension=0, tiled=True)
    inv_degree = 1.0 / degree.astype(jnp.float32)
    aggregate = (agg_sum * inv_degree[:, None]).astype(jnp.bfloat16)
    before = (
        jnp.dot(features, w_self, preferred_element_type=jnp.float32)
        + jnp.dot(aggregate, w_neigh, preferred_element_type=jnp.float32)
        + layer_bias
    )
    hidden = gelu_value(before).astype(jnp.bfloat16)
    first_node = (lax.axis_index("row") * col_count + lax.axis_index("col")) * node_rows
    node_ids = first_node + jnp.arange(node_rows, dtype=jnp.int32)
    target = jnp.any(node_ids[:, None] == target_ids[None, :], axis=1).astype(jnp.float32)
    slope_grad = (cotangent.astype(jnp.float32) * target[:, None] * gelu_slope(before)).astype(
        jnp.bfloat16
    )
    grad_scale = 1.0 / math.sqrt(node_rows * row_count * col_count)
    contract_rows = (((0,), (0,)), ((), ()))
    self_term = lax.dot_general(
        features, slope_grad, contract_rows, preferred_element_type=jnp.float32
    )
    neigh_term = lax.dot_general(
        aggregate, slope_grad, contract_rows, preferred_element_type=jnp.float32
    )
    bias_term = jnp.sum(slope_grad.astype(jnp.float32), axis=0)
    self_sum, neigh_sum, bias_sum = lax.psum((self_term, neigh_term, bias_term), ("row", "col"))
    contract_out = (((1,), (1,)), ((), ()))
    message = (
        lax.dot_general(slope_grad, w_neigh, contract_out, preferred_element_type=jnp.float32)
        * inv_degree[:, None]
    ).astype(jnp.bfloat16)
    message_slab = lax.all_gather(message, "col", axis=0, tiled=True)
    back_part = tile_sum(
        cell_tiles,
        cell_dst,
        cell_src,
        usable,
        message_slab,
        row_count * node_rows // tile_width,
        True,
        0,
    )
    neighbour_grad = lax.psum_scatter(
        back_part.astype(jnp.bfloat16).astype(jnp.float32).astype(jnp.bfloat16),
        "row",
        scatter_dimension=0,
        tiled=True,
    ).astype(jnp.float32)
    direct = lax.dot_general(slope_grad, w_self, contract_out, preferred_element_type=jnp.float32)
    grad_features = (direct + neighbour_grad).astype(jnp.bfloat16)
    return (
        hidden,
        grad_features,
        self_sum * grad_scale,
        neigh_sum * grad_scale,
        bias_sum * grad_scale,
    )


def solution(mesh):
    in_specs = (
        P(("groups", "row", "col"), None),
        P(),
        P(),
        P(),
        P(("groups", "row"), "col", None, None, None),
        P(("groups", "row"), "col", None),
        P(("groups", "row"), "col", None),
        P(("groups", "row"), "col"),
        P(("groups", "row", "col")),
        P("groups"),
        P(("groups", "row", "col"), None),
    )
    out_specs = (
        P(("groups", "row", "col"), None),
        P(("groups", "row", "col"), None),
        P("groups", None),
        P("groups", None),
        P("groups"),
    )
    four = mesh.shape["row"] == 4 and mesh.shape["col"] == 4

    def per_device(*args):
        tiles_are_owned_blocks = args[0].shape[0] == args[4].shape[-1] == 128
        return (compact_device if four and tiles_are_owned_blocks else dense_device)(*args)

    return jax.shard_map(
        per_device, mesh=mesh, in_specs=in_specs, out_specs=out_specs, check_vma=False
    )
```

```python
import functools
import itertools
import math

import jax
import jax.numpy as jnp
from jax import lax
from jax.experimental import pallas as pl
from jax.experimental.pallas import tpu as pltpu
from jax.sharding import PartitionSpec as P

F32 = jnp.float32
BF16 = jnp.bfloat16


def gelu_value(inputs):
    return 0.5 * inputs * (1.0 + jax.scipy.special.erf(inputs * 0.7071067811865476))


def gelu_slope(inputs):
    return (
        0.5 * (1.0 + jax.scipy.special.erf(inputs * 0.7071067811865476))
        + inputs * jnp.exp(-0.5 * inputs * inputs) * 0.3989422804014327
    )


def dot(left, right, dims=((1,), (0,))):
    return lax.dot_general(left, right, (dims, ((), ())), preferred_element_type=F32)


def trade(block, axis, step):
    return lax.ppermute(block, axis, [(i, i ^ step) for i in range(lax.axis_size(axis))])


def swap_quarters(line):
    first, second, third, last = jnp.split(line, 4, axis=1)
    return jnp.concatenate([first, third, second, last], axis=1)


def flip(line, parts, bit):
    cut = jnp.split(line, parts, axis=1)
    turned = [cut[i ^ 1] for i in range(parts)]
    return jnp.where(bit == 1, jnp.concatenate(turned, axis=1), line)


MERGE_COST = pl.CostEstimate(flops=2 * 10**9, bytes_accessed=0, transcendentals=0)
DENSE_COST = pl.CostEstimate(flops=3 * 10**9, bytes_accessed=0, transcendentals=0)


def call(kernel, outputs, *inputs, spaces=(), scratch=(), out_space=pltpu.VMEM, cost=None):
    inputs = [
        pltpu.with_memory_space_constraint(x, y) if y == pltpu.HBM else x
        for x, y in itertools.zip_longest(inputs, spaces)
    ]
    spaces = list(spaces) + [pltpu.VMEM] * (len(inputs) - len(spaces))
    return pl.pallas_call(
        kernel,
        out_shape=[jax.ShapeDtypeStruct(shape, dtype) for shape, dtype in outputs],
        in_specs=[pl.BlockSpec(memory_space=space) for space in spaces],
        out_specs=[pl.BlockSpec(memory_space=out_space) for _ in outputs],
        scratch_shapes=scratch,
        cost_estimate=cost,
        compiler_params=pltpu.CompilerParams(vmem_limit_bytes=32 * 2**20),
    )(*inputs)


def spread(block, axis, steps):
    return {step: trade(block, axis, step) for step in steps}


def swap_bits(index):
    return index // 2 + index % 2 * 2


def select(rows, cols, ids_in, src_in, dst_in, count_in, tiles_in, cotangent_in, degree_in, *refs):
    weights_in, refs = refs[:4], refs[4:]
    adjacency, column_picks, own_picks, known, near, far, inverse, *refs = refs
    weights, (picks, src, dst, count, tiles, cotangent, degree, ids, sems) = refs[:4], refs[4:]
    pairs = [(ids_in, ids), (cotangent_in, cotangent), (degree_in, degree), (tiles_in, tiles)]
    pairs += [(src_in, src), (dst_in, dst), (count_in, count)]
    pairs += list(zip(weights_in, weights))
    copies = [pltpu.make_async_copy(a, b, sems.at[i]) for i, (a, b) in enumerate(pairs)]
    for copy in copies:
        copy.start()
    row, col = lax.axis_index("row"), lax.axis_index("col")
    slots, (nodes, width) = ids.shape[1], cotangent.shape
    adjacency[...] = jnp.zeros(adjacency.shape, adjacency.dtype)
    copies[0].wait()
    line = flip(flip(swap_quarters(ids[...]), 2, col % 2), 4, col // 2)
    line = jnp.broadcast_to(line, (nodes, slots))
    stack = line.T
    lanes = lax.broadcasted_iota(jnp.int32, (slots, nodes), 1)
    for k in range(cols):
        base = (row * cols + (col ^ swap_bits(k))) * nodes
        picks[:, k * nodes : (k + 1) * nodes] = (stack == lanes + base).astype(BF16)
    for s in range(rows):
        base = ((row ^ s) * cols + col) * nodes
        column_picks[:, s * nodes : (s + 1) * nodes] = (stack == lanes + base).astype(BF16)
    base = (row * cols + col) * nodes
    across = lax.broadcasted_iota(jnp.int32, (nodes, slots), 0)
    own_picks[...] = (line == across + base).astype(BF16)
    for copy in copies[1:3]:
        copy.wait()
    own = picks[:, :nodes]
    known[:, :width] = dot(own, cotangent[...]).astype(BF16)
    counts = degree[...].astype(F32)
    inverse[...] = 1.0 / jnp.broadcast_to(counts, (nodes, nodes)).T
    counts = jnp.sum(own.astype(F32) * counts, axis=1, keepdims=True)
    known[:, width:] = jnp.broadcast_to(counts, (slots, 128)).astype(BF16)
    for copy in copies[3:]:
        copy.wait()
    for k in range(tiles.shape[2]):

        @pl.when(k < count[0, 0])
        def _():
            down = pl.multiple_of(swap_bits(dst[0, 0, k] ^ col) * nodes, nodes)
            across = pl.multiple_of((src[0, 0, k] ^ row) * nodes, nodes)
            adjacency[pl.ds(down, nodes), pl.ds(across, nodes)] = tiles[0, 0, k]

    picked = dot(picks[...], adjacency[...]).astype(BF16)
    for s in range(rows):
        block = picked[:, s * nodes : (s + 1) * nodes]
        (far if s // 2 else near)[s % 2 * slots : (s % 2 + 1) * slots, :] = block


def block_of(step, near, far, slots):
    return (far if step // 2 else near)[step % 2 * slots : (step % 2 + 1) * slots, :]


def dense_part(steps, adjacency, *refs):
    *features, kept, sent = refs
    nodes = features[0].shape[0]
    total = sum(
        dot(adjacency[:, step * nodes : (step + 1) * nodes], block[...])
        for step, block in zip(steps, features)
    )
    half = kept.shape[0]
    kept[...] = total[:half]
    sent[...] = total[half:].astype(BF16)


def combine(steps, column_picks, known, *refs):
    features, (near, far, sent, part, fixed) = refs[: len(steps)], refs[len(steps) :]
    nodes, width = features[0].shape
    half = part.shape[0]
    sums, picked = 0.0, 0.0
    for step, block in zip(steps, features):
        sums += dot(block_of(step, near, far, 2 * half), block[...])
        picked += dot(column_picks[:, step * nodes : (step + 1) * nodes], block[...])
    picked = picked.astype(BF16)
    part[...] = sums[:half]
    fixed[:, :width] = picked[:half]
    fixed[:, width:] = known[:half, :]
    sent[:, :width] = sums[half:].astype(BF16)
    sent[:, width : 2 * width] = picked[half:]
    sent[:, 2 * width :] = known[half:, :]


def relay(part, fixed, got, sent, part_out, fixed_out):
    share, width = part_out.shape
    sums = part[...] + got[:, :width].astype(F32)
    rest = fixed[...] + got[:, width:]
    part_out[...] = sums[:share]
    fixed_out[...] = rest[:share]
    sent[:, :width] = sums[share:].astype(BF16)
    sent[:, width:] = rest[share:]


def slopes(part, fixed, got, w_self, w_neigh, layer_bias, found, features):
    width = part.shape[1]
    total = part[...] + got[:, :width].astype(F32)
    rest = fixed[...] + got[:, width:]
    features[...] = rest[:, :width]
    cotangent = rest[:, width : 2 * width].astype(F32)
    degrees = rest[:, 2 * width :]
    degree = degrees[:, :1].astype(F32)
    inverse = jnp.where(degree > 0, 1.0 / jnp.maximum(degree, 1.0), 0.0)
    aggregate = (total * inverse).astype(BF16)
    before = dot(rest[:, :width], w_self[...]) + dot(aggregate, w_neigh[...]) + layer_bias[...]
    slope = (cotangent * gelu_slope(before)).astype(BF16)
    share, bands = part.shape[0], width // 128
    for b in range(bands):
        found[b * share : (b + 1) * share, :] = slope[:, b * 128 : (b + 1) * 128]
        down = (bands + b) * share
        found[down : down + share, :] = aggregate[:, b * 128 : (b + 1) * 128]
    line = degrees.astype(F32).T[:16, :]
    line = jnp.concatenate([line, jnp.zeros((16, 128 - share), F32)], axis=1)
    found[2 * bands * share :, :] = line.astype(BF16)


def merge(*refs):
    refs[-1][...] = sum(part[...] for part in refs[:-1])


def activate(features, total, got, inverse, w_self, w_neigh, layer_bias, hidden):
    total = total[...] + got[...].astype(F32)
    aggregate = (total * inverse[:, :1]).astype(BF16)
    before = dot(features[...], w_self[...]) + dot(aggregate, w_neigh[...]) + layer_bias[...]
    hidden[...] = gelu_value(before).astype(BF16)


def finish(scale, *refs):
    found, features, refs = refs[:2], refs[2:4], refs[4:]
    own_columns, own_picks, w_self, w_neigh, *refs = refs
    outs, (slope, aggregate, *results, sems) = refs[:4], refs[4:]
    grad_features, grad_self, grad_neigh, grad_bias = results
    slots, width = slope.shape
    half, bands = slots // 2, width // 128
    share = half // 2
    size = found[0].shape[0] // 2
    front, back = ((0,), (0,)), ((1,), (1,))
    degrees = []
    for q in range(4):
        part, base, here = found[q // 2], q % 2 * size, slice(q * share, (q + 1) * share)
        for b in range(bands):
            lanes = slice(b * 128, (b + 1) * 128)
            slope[here, lanes] = part[base + b * share : base + (b + 1) * share, :]
            down = base + (bands + b) * share
            aggregate[here, lanes] = part[down : down + share, :]
        degrees.append(part[base + size - 16 : base + size, :].astype(F32)[:1, :share])
    copies = [pltpu.make_async_copy(a, b, sems.at[i]) for i, (a, b) in enumerate(zip(results, outs))]
    grad_self[...] = scale * (
        dot(features[0][...], slope[:half, :], front)
        + dot(features[1][...], slope[half:, :], front)
    )
    copies[1].start()
    grad_neigh[...] = dot(aggregate[...], slope[...], front) * scale
    copies[2].start()
    grad_bias[...] = jnp.sum(slope[...].astype(F32), axis=0, keepdims=True) * scale
    copies[3].start()
    degree = jnp.broadcast_to(jnp.concatenate(degrees, axis=1), (128, slots)).T[:, :1]
    message = (dot(slope[...], w_neigh[...], back) / degree).astype(BF16)
    own_slope = dot(own_picks[...], slope[...]).astype(BF16)
    total = dot(own_slope, w_self[...], back) + dot(own_columns[...], message, front)
    grad_features[...] = total.astype(BF16)
    copies[0].start()
    for copy in copies:
        copy.wait()


def compact_device(
    features,
    w_self,
    w_neigh,
    layer_bias,
    tile_vals,
    tile_dst,
    tile_src,
    tile_count,
    degree,
    target_ids,
    cotangent,
):
    rows = lax.axis_size("row")
    cols = lax.axis_size("col")
    nodes, width = features.shape
    slots = target_ids.shape[0]
    share = slots // cols
    half = slots // 2

    order = (3, 1, 2)
    feature_parts = spread(features, "row", order)

    bias = layer_bias.reshape(1, width)
    adjacency, column_picks, own_picks, known, near, far, inverse, *resident = call(
        functools.partial(select, rows, cols),
        [
            ((cols * nodes, rows * nodes), BF16),
            ((slots, rows * nodes), BF16),
            ((nodes, slots), BF16),
            ((slots, width + 128), BF16),
        ]
        + [((rows // 2 * slots, nodes), BF16)] * 2
        + [((nodes, nodes), F32)]
        + [((width, width), BF16)] * 2
        + [((1, width), F32), ((nodes, width), BF16)],
        target_ids.reshape(1, slots),
        tile_src,
        tile_dst,
        tile_count,
        tile_vals,
        cotangent,
        degree.reshape(1, nodes),
        w_self,
        w_neigh,
        bias,
        features,
        spaces=[pltpu.HBM] * 3 + [pl.ANY] + [pltpu.HBM] * 7,
        scratch=[pltpu.VMEM((slots, cols * nodes), BF16)]
        + [pltpu.SMEM(x.shape, x.dtype) for x in (tile_src, tile_dst, tile_count)]
        + [pltpu.VMEM(x.shape, x.dtype) for x in (tile_vals, cotangent)]
        + [pltpu.VMEM((1, nodes), jnp.int32), pltpu.VMEM((1, slots), jnp.int32)]
        + [pltpu.SemaphoreType.DMA((11,))],
    )
    w_self, w_neigh, bias, features = resident
    feature_parts[0] = features
    sent, part, fixed = call(
        functools.partial(combine, order + (0,)),
        [((half, 3 * width + 128), BF16), ((half, width), F32), ((half, 2 * width + 128), BF16)],
        column_picks,
        known,
        *[feature_parts[step] for step in order + (0,)],
        near,
        far,
    )
    got = trade(sent, "col", 1)
    sent, part, fixed = call(
        relay,
        [((share, 3 * width + 128), BF16), ((share, width), F32), ((share, 2 * width + 128), BF16)],
        part,
        fixed,
        got,
    )
    got = trade(sent, "col", 2)
    found, feature_slots = call(
        slopes,
        [((2 * (width // 128) * share + 16, 128), BF16), ((share, width), BF16)],
        part,
        fixed,
        got,
        w_self,
        w_neigh,
        bias,
    )
    columns = near + trade(far, "row", 2)
    found, columns = lax.optimization_barrier((found, columns))
    dense, dense_sent = call(
        functools.partial(dense_part, order + (0,)),
        [((2 * nodes, width), F32), ((2 * nodes, width), BF16)],
        adjacency,
        *[feature_parts[step] for step in order + (0,)],
        cost=DENSE_COST,
    )
    dense = dense + trade(dense_sent, "col", 1).astype(F32)
    parts = spread(found, "row", order)
    (found,) = call(merge, [(found.shape, BF16)], parts.pop(order[0]), found, cost=MERGE_COST)
    found, feature_slots = lax.optimization_barrier((found, feature_slots))
    found, dense = lax.optimization_barrier((found, dense))
    (found,) = call(merge, [(found.shape, BF16)], *parts.values(), found, cost=MERGE_COST)
    own_columns = columns[:slots] + trade(columns[slots:], "row", 1)
    dense_got = trade(dense[nodes:].astype(BF16), "col", 2)
    feature_mine = jnp.concatenate([feature_slots, trade(feature_slots, "col", 2)], axis=0)
    feature_other = trade(feature_mine, "col", 1)
    found_mine = jnp.concatenate([found, trade(found, "col", 2)], axis=0)
    found_other = trade(found_mine, "col", 1)
    (hidden,) = call(
        activate,
        [((nodes, width), BF16)],
        features,
        dense[:nodes],
        dense_got,
        inverse,
        w_self,
        w_neigh,
        bias,
    )
    results = [((nodes, width), BF16), ((width, width), F32), ((width, width), F32), ((1, width), F32)]
    grad_features, grad_self, grad_neigh, grad_bias = call(
        functools.partial(finish, 1.0 / math.sqrt(nodes * rows * cols)),
        results,
        found_mine,
        found_other,
        feature_mine,
        feature_other,
        own_columns,
        own_picks,
        w_self,
        w_neigh,
        scratch=[pltpu.VMEM((slots, width), BF16)] * 2
        + [pltpu.VMEM(*result) for result in results]
        + [pltpu.SemaphoreType.DMA((4,))],
        out_space=pl.ANY,
    )
    return (hidden, grad_features, grad_self, grad_neigh, grad_bias.reshape(width))


def tile_sum(values, take_index, put_index, usable, source, out_tiles, transpose, first_tile):
    slot_count, tile_width = (values.shape[0], values.shape[1])
    columns = source.shape[1]
    blocks = source.reshape(-1, tile_width, columns)
    group_size = math.gcd(slot_count, 16)
    pattern = "kji,kjf->kif" if transpose else "kij,kjf->kif"

    def advance(running, offset):
        tile_block = lax.dynamic_slice_in_dim(values, offset, group_size, 0)
        taken = lax.dynamic_slice_in_dim(take_index, offset, group_size, 0)
        placed = lax.dynamic_slice_in_dim(put_index, offset, group_size, 0) - first_tile
        allowed = lax.dynamic_slice_in_dim(usable, offset, group_size, 0)
        inside = allowed & (placed >= 0) & (placed < out_tiles)
        chosen = blocks[taken]
        product = jnp.einsum(pattern, tile_block, chosen, preferred_element_type=jnp.float32)
        product = product * inside.astype(jnp.float32)[:, None, None]
        where_to = jnp.where(inside, placed, 0)
        running = running.at[where_to].add(product)
        return (running, None)

    offsets = jnp.arange(0, slot_count, group_size, dtype=jnp.int32)
    running, _ = lax.scan(
        advance, jnp.zeros((out_tiles, tile_width, columns), jnp.float32), offsets
    )
    return running.reshape(out_tiles * tile_width, columns)


def dense_device(
    features,
    w_self,
    w_neigh,
    layer_bias,
    tile_vals,
    tile_dst,
    tile_src,
    tile_count,
    degree,
    target_ids,
    cotangent,
):
    row_count = lax.axis_size("row")
    col_count = lax.axis_size("col")
    node_rows = features.shape[0]
    tile_width = tile_vals.shape[-1]
    cell_tiles = tile_vals[0, 0]
    cell_dst = tile_dst[0, 0]
    cell_src = tile_src[0, 0]
    usable = jnp.arange(cell_tiles.shape[0], dtype=jnp.int32) < tile_count[0, 0]
    source = lax.all_gather(features, "row", axis=0, tiled=True)
    partial_value = tile_sum(
        cell_tiles,
        cell_src,
        cell_dst,
        usable,
        source,
        col_count * node_rows // tile_width,
        False,
        0,
    )
    agg_sum = lax.psum_scatter(partial_value, "col", scatter_dimension=0, tiled=True)
    inv_degree = 1.0 / degree.astype(jnp.float32)
    aggregate = (agg_sum * inv_degree[:, None]).astype(jnp.bfloat16)
    before = (
        jnp.dot(features, w_self, preferred_element_type=jnp.float32)
        + jnp.dot(aggregate, w_neigh, preferred_element_type=jnp.float32)
        + layer_bias
    )
    hidden = gelu_value(before).astype(jnp.bfloat16)
    first_node = (lax.axis_index("row") * col_count + lax.axis_index("col")) * node_rows
    node_ids = first_node + jnp.arange(node_rows, dtype=jnp.int32)
    target = jnp.any(node_ids[:, None] == target_ids[None, :], axis=1).astype(jnp.float32)
    slope_grad = (cotangent.astype(jnp.float32) * target[:, None] * gelu_slope(before)).astype(
        jnp.bfloat16
    )
    grad_scale = 1.0 / math.sqrt(node_rows * row_count * col_count)
    contract_rows = (((0,), (0,)), ((), ()))
    self_term = lax.dot_general(
        features, slope_grad, contract_rows, preferred_element_type=jnp.float32
    )
    neigh_term = lax.dot_general(
        aggregate, slope_grad, contract_rows, preferred_element_type=jnp.float32
    )
    bias_term = jnp.sum(slope_grad.astype(jnp.float32), axis=0)
    self_sum, neigh_sum, bias_sum = lax.psum((self_term, neigh_term, bias_term), ("row", "col"))
    contract_out = (((1,), (1,)), ((), ()))
    message = (
        lax.dot_general(slope_grad, w_neigh, contract_out, preferred_element_type=jnp.float32)
        * inv_degree[:, None]
    ).astype(jnp.bfloat16)
    message_slab = lax.all_gather(message, "col", axis=0, tiled=True)
    back_part = tile_sum(
        cell_tiles,
        cell_dst,
        cell_src,
        usable,
        message_slab,
        row_count * node_rows // tile_width,
        True,
        0,
    )
    neighbour_grad = lax.psum_scatter(
        back_part.astype(jnp.bfloat16).astype(jnp.float32).astype(jnp.bfloat16),
        "row",
        scatter_dimension=0,
        tiled=True,
    ).astype(jnp.float32)
    direct = lax.dot_general(slope_grad, w_self, contract_out, preferred_element_type=jnp.float32)
    grad_features = (direct + neighbour_grad).astype(jnp.bfloat16)
    return (
        hidden,
        grad_features,
        self_sum * grad_scale,
        neigh_sum * grad_scale,
        bias_sum * grad_scale,
    )


def solution(mesh):
    in_specs = (
        P(("groups", "row", "col"), None),
        P(),
        P(),
        P(),
        P(("groups", "row"), "col", None, None, None),
        P(("groups", "row"), "col", None),
        P(("groups", "row"), "col", None),
        P(("groups", "row"), "col"),
        P(("groups", "row", "col")),
        P("groups"),
        P(("groups", "row", "col"), None),
    )
    out_specs = (
        P(("groups", "row", "col"), None),
        P(("groups", "row", "col"), None),
        P("groups", None),
        P("groups", None),
        P("groups"),
    )
    four = mesh.shape["row"] == 4 and mesh.shape["col"] == 4

    def per_device(*args):
        tiles_are_owned_blocks = args[0].shape[0] == args[4].shape[-1] == 128
        return (compact_device if four and tiles_are_owned_blocks else dense_device)(*args)

    return jax.shard_map(
        per_device, mesh=mesh, in_specs=in_specs, out_specs=out_specs, check_vma=False
    )
```

```python
import functools
import itertools
import math

import jax
import jax.numpy as jnp
from jax import lax
from jax.experimental import pallas as pl
from jax.experimental.pallas import tpu as pltpu
from jax.sharding import PartitionSpec as P

F32 = jnp.float32
BF16 = jnp.bfloat16


def gelu_value(inputs):
    return 0.5 * inputs * (1.0 + jax.scipy.special.erf(inputs * 0.7071067811865476))


def gelu_slope(inputs):
    return (
        0.5 * (1.0 + jax.scipy.special.erf(inputs * 0.7071067811865476))
        + inputs * jnp.exp(-0.5 * inputs * inputs) * 0.3989422804014327
    )


def dot(left, right, dims=((1,), (0,))):
    return lax.dot_general(left, right, (dims, ((), ())), preferred_element_type=F32)


def trade(block, axis, step):
    return lax.ppermute(block, axis, [(i, i ^ step) for i in range(lax.axis_size(axis))])


def swap_quarters(line):
    first, second, third, last = jnp.split(line, 4, axis=1)
    return jnp.concatenate([first, third, second, last], axis=1)


def flip(line, parts, bit):
    cut = jnp.split(line, parts, axis=1)
    turned = [cut[i ^ 1] for i in range(parts)]
    return jnp.where(bit == 1, jnp.concatenate(turned, axis=1), line)


MERGE_COST = pl.CostEstimate(flops=2 * 10**9, bytes_accessed=0, transcendentals=0)
DENSE_COST = pl.CostEstimate(flops=3 * 10**9, bytes_accessed=0, transcendentals=0)


def call(kernel, outputs, *inputs, spaces=(), scratch=(), out_space=pltpu.VMEM, cost=None):
    inputs = [
        pltpu.with_memory_space_constraint(x, y) if y == pltpu.HBM else x
        for x, y in itertools.zip_longest(inputs, spaces)
    ]
    spaces = list(spaces) + [pltpu.VMEM] * (len(inputs) - len(spaces))
    return pl.pallas_call(
        kernel,
        out_shape=[jax.ShapeDtypeStruct(shape, dtype) for shape, dtype in outputs],
        in_specs=[pl.BlockSpec(memory_space=space) for space in spaces],
        out_specs=[pl.BlockSpec(memory_space=out_space) for _ in outputs],
        scratch_shapes=scratch,
        cost_estimate=cost,
        compiler_params=pltpu.CompilerParams(vmem_limit_bytes=32 * 2**20),
    )(*inputs)


def spread(block, axis, steps):
    return {step: trade(block, axis, step) for step in steps}


def swap_bits(index):
    return index // 2 + index % 2 * 2


def select(rows, cols, ids_in, src_in, dst_in, count_in, tiles_in, cotangent_in, degree_in, *refs):
    weights_in, refs = refs[:4], refs[4:]
    adjacency, column_picks, own_picks, known, near, far, inverse, *refs = refs
    weights, (picks, src, dst, count, tiles, cotangent, degree, ids, sems) = refs[:4], refs[4:]
    pairs = [(ids_in, ids), (cotangent_in, cotangent), (degree_in, degree), (tiles_in, tiles)]
    pairs += [(src_in, src), (dst_in, dst), (count_in, count)]
    pairs += list(zip(weights_in, weights))
    copies = [pltpu.make_async_copy(a, b, sems.at[i]) for i, (a, b) in enumerate(pairs)]
    for copy in copies:
        copy.start()
    row, col = lax.axis_index("row"), lax.axis_index("col")
    slots, (nodes, width) = ids.shape[1], cotangent.shape
    adjacency[...] = jnp.zeros(adjacency.shape, adjacency.dtype)
    copies[0].wait()
    line = flip(flip(swap_quarters(ids[...]), 2, col % 2), 4, col // 2)
    line = jnp.broadcast_to(line, (nodes, slots))
    stack = line.T
    lanes = lax.broadcasted_iota(jnp.int32, (slots, nodes), 1)
    for k in range(cols):
        base = (row * cols + (col ^ swap_bits(k))) * nodes
        picks[:, k * nodes : (k + 1) * nodes] = (stack == lanes + base).astype(BF16)
    for s in range(rows):
        base = ((row ^ s) * cols + col) * nodes
        column_picks[:, s * nodes : (s + 1) * nodes] = (stack == lanes + base).astype(BF16)
    base = (row * cols + col) * nodes
    across = lax.broadcasted_iota(jnp.int32, (nodes, slots), 0)
    own_picks[...] = (line == across + base).astype(BF16)
    for copy in copies[1:3]:
        copy.wait()
    own = picks[:, :nodes]
    known[:, :width] = dot(own, cotangent[...]).astype(BF16)
    counts = degree[...].astype(F32)
    inverse[...] = 1.0 / jnp.broadcast_to(counts, (nodes, nodes)).T
    counts = jnp.sum(own.astype(F32) * counts, axis=1, keepdims=True)
    known[:, width:] = jnp.broadcast_to(counts, (slots, 128)).astype(BF16)
    for copy in copies[3:7]:
        copy.wait()
    for k in range(tiles.shape[2]):

        @pl.when(k < count[0, 0])
        def _():
            down = pl.multiple_of(swap_bits(dst[0, 0, k] ^ col) * nodes, nodes)
            across = pl.multiple_of((src[0, 0, k] ^ row) * nodes, nodes)
            adjacency[pl.ds(down, nodes), pl.ds(across, nodes)] = tiles[0, 0, k]

    picked = dot(picks[...], adjacency[...]).astype(BF16)
    for s in range(rows):
        block = picked[:, s * nodes : (s + 1) * nodes]
        (far if s // 2 else near)[s % 2 * slots : (s % 2 + 1) * slots, :] = block
    for copy in copies[7:]:
        copy.wait()


def block_of(step, near, far, slots):
    return (far if step // 2 else near)[step % 2 * slots : (step % 2 + 1) * slots, :]


def dense_part(steps, adjacency, *refs):
    *features, kept, sent = refs
    nodes = features[0].shape[0]
    total = sum(
        dot(adjacency[:, step * nodes : (step + 1) * nodes], block[...])
        for step, block in zip(steps, features)
    )
    half = kept.shape[0]
    kept[...] = total[:half]
    sent[...] = total[half:].astype(BF16)


def combine(steps, column_picks, known, *refs):
    features, (near, far, sent, part, fixed) = refs[: len(steps)], refs[len(steps) :]
    nodes, width = features[0].shape
    half = part.shape[0]
    sums, picked = 0.0, 0.0
    for step, block in zip(steps, features):
        sums += dot(block_of(step, near, far, 2 * half), block[...])
        picked += dot(column_picks[:, step * nodes : (step + 1) * nodes], block[...])
    picked = picked.astype(BF16)
    part[...] = sums[:half]
    fixed[:, :width] = picked[:half]
    fixed[:, width:] = known[:half, :]
    sent[:, :width] = sums[half:].astype(BF16)
    sent[:, width : 2 * width] = picked[half:]
    sent[:, 2 * width :] = known[half:, :]


def relay(part, fixed, got, sent, part_out, fixed_out):
    share, width = part_out.shape
    sums = part[...] + got[:, :width].astype(F32)
    rest = fixed[...] + got[:, width:]
    part_out[...] = sums[:share]
    fixed_out[...] = rest[:share]
    sent[:, :width] = sums[share:].astype(BF16)
    sent[:, width:] = rest[share:]


def slopes(part, fixed, got, w_self, w_neigh, layer_bias, found, features):
    width = part.shape[1]
    total = part[...] + got[:, :width].astype(F32)
    rest = fixed[...] + got[:, width:]
    features[...] = rest[:, :width]
    cotangent = rest[:, width : 2 * width].astype(F32)
    degrees = rest[:, 2 * width :]
    degree = degrees[:, :1].astype(F32)
    inverse = jnp.where(degree > 0, 1.0 / jnp.maximum(degree, 1.0), 0.0)
    aggregate = (total * inverse).astype(BF16)
    before = dot(rest[:, :width], w_self[...]) + dot(aggregate, w_neigh[...]) + layer_bias[...]
    slope = (cotangent * gelu_slope(before)).astype(BF16)
    share, bands = part.shape[0], width // 128
    for b in range(bands):
        found[b * share : (b + 1) * share, :] = slope[:, b * 128 : (b + 1) * 128]
        down = (bands + b) * share
        found[down : down + share, :] = aggregate[:, b * 128 : (b + 1) * 128]
    line = degrees.astype(F32).T[:16, :]
    line = jnp.concatenate([line, jnp.zeros((16, 128 - share), F32)], axis=1)
    found[2 * bands * share :, :] = line.astype(BF16)


def merge(*refs):
    refs[-1][...] = sum(part[...] for part in refs[:-1])


def activate(features, total, got, inverse, w_self, w_neigh, layer_bias, hidden):
    total = total[...] + got[...].astype(F32)
    aggregate = (total * inverse[:, :1]).astype(BF16)
    before = dot(features[...], w_self[...]) + dot(aggregate, w_neigh[...]) + layer_bias[...]
    hidden[...] = gelu_value(before).astype(BF16)


def finish(scale, *refs):
    found, features, refs = refs[:2], refs[2:4], refs[4:]
    own_columns, own_picks, w_self, w_neigh, *refs = refs
    outs, (slope, aggregate, *results, sems) = refs[:4], refs[4:]
    grad_features, grad_self, grad_neigh, grad_bias = results
    slots, width = slope.shape
    half, bands = slots // 2, width // 128
    share = half // 2
    size = found[0].shape[0] // 2
    front, back = ((0,), (0,)), ((1,), (1,))
    degrees = []
    for q in range(4):
        part, base, here = found[q // 2], q % 2 * size, slice(q * share, (q + 1) * share)
        for b in range(bands):
            lanes = slice(b * 128, (b + 1) * 128)
            slope[here, lanes] = part[base + b * share : base + (b + 1) * share, :]
            down = base + (bands + b) * share
            aggregate[here, lanes] = part[down : down + share, :]
        degrees.append(part[base + size - 16 : base + size, :].astype(F32)[:1, :share])
    copies = [pltpu.make_async_copy(a, b, sems.at[i]) for i, (a, b) in enumerate(zip(results, outs))]
    grad_self[...] = scale * (
        dot(features[0][...], slope[:half, :], front)
        + dot(features[1][...], slope[half:, :], front)
    )
    copies[1].start()
    grad_neigh[...] = dot(aggregate[...], slope[...], front) * scale
    copies[2].start()
    grad_bias[...] = jnp.sum(slope[...].astype(F32), axis=0, keepdims=True) * scale
    copies[3].start()
    degree = jnp.broadcast_to(jnp.concatenate(degrees, axis=1), (128, slots)).T[:, :1]
    message = (dot(slope[...], w_neigh[...], back) / degree).astype(BF16)
    own_slope = dot(own_picks[...], slope[...]).astype(BF16)
    total = dot(own_slope, w_self[...], back) + dot(own_columns[...], message, front)
    grad_features[...] = total.astype(BF16)
    copies[0].start()
    for copy in copies:
        copy.wait()


def compact_device(
    features,
    w_self,
    w_neigh,
    layer_bias,
    tile_vals,
    tile_dst,
    tile_src,
    tile_count,
    degree,
    target_ids,
    cotangent,
):
    rows = lax.axis_size("row")
    cols = lax.axis_size("col")
    nodes, width = features.shape
    slots = target_ids.shape[0]
    share = slots // cols
    half = slots // 2

    order = (3, 1, 2)
    feature_parts = spread(features, "row", order)

    bias = layer_bias.reshape(1, width)
    adjacency, column_picks, own_picks, known, near, far, inverse, *resident = call(
        functools.partial(select, rows, cols),
        [
            ((cols * nodes, rows * nodes), BF16),
            ((slots, rows * nodes), BF16),
            ((nodes, slots), BF16),
            ((slots, width + 128), BF16),
        ]
        + [((rows // 2 * slots, nodes), BF16)] * 2
        + [((nodes, nodes), F32)]
        + [((width, width), BF16)] * 2
        + [((1, width), F32), ((nodes, width), BF16)],
        target_ids.reshape(1, slots),
        tile_src,
        tile_dst,
        tile_count,
        tile_vals,
        cotangent,
        degree.reshape(1, nodes),
        w_self,
        w_neigh,
        bias,
        features,
        spaces=[pltpu.HBM] * 3 + [pl.ANY] + [pltpu.HBM] * 7,
        scratch=[pltpu.VMEM((slots, cols * nodes), BF16)]
        + [pltpu.SMEM(x.shape, x.dtype) for x in (tile_src, tile_dst, tile_count)]
        + [pltpu.VMEM(x.shape, x.dtype) for x in (tile_vals, cotangent)]
        + [pltpu.VMEM((1, nodes), jnp.int32), pltpu.VMEM((1, slots), jnp.int32)]
        + [pltpu.SemaphoreType.DMA((11,))],
    )
    w_self, w_neigh, bias, features = resident
    feature_parts[0] = features
    sent, part, fixed = call(
        functools.partial(combine, order + (0,)),
        [((half, 3 * width + 128), BF16), ((half, width), F32), ((half, 2 * width + 128), BF16)],
        column_picks,
        known,
        *[feature_parts[step] for step in order + (0,)],
        near,
        far,
    )
    got = trade(sent, "col", 1)
    sent, part, fixed = call(
        relay,
        [((share, 3 * width + 128), BF16), ((share, width), F32), ((share, 2 * width + 128), BF16)],
        part,
        fixed,
        got,
    )
    got = trade(sent, "col", 2)
    found, feature_slots = call(
        slopes,
        [((2 * (width // 128) * share + 16, 128), BF16), ((share, width), BF16)],
        part,
        fixed,
        got,
        w_self,
        w_neigh,
        bias,
    )
    columns = near + trade(far, "row", 2)
    found, columns = lax.optimization_barrier((found, columns))
    dense, dense_sent = call(
        functools.partial(dense_part, order + (0,)),
        [((2 * nodes, width), F32), ((2 * nodes, width), BF16)],
        adjacency,
        *[feature_parts[step] for step in order + (0,)],
        cost=DENSE_COST,
    )
    dense = dense + trade(dense_sent, "col", 1).astype(F32)
    parts = spread(found, "row", order)
    (found,) = call(merge, [(found.shape, BF16)], parts.pop(order[0]), found, cost=MERGE_COST)
    found, feature_slots = lax.optimization_barrier((found, feature_slots))
    found, dense = lax.optimization_barrier((found, dense))
    (found,) = call(merge, [(found.shape, BF16)], *parts.values(), found, cost=MERGE_COST)
    own_columns = columns[:slots] + trade(columns[slots:], "row", 1)
    dense_got = trade(dense[nodes:].astype(BF16), "col", 2)
    feature_mine = jnp.concatenate([feature_slots, trade(feature_slots, "col", 2)], axis=0)
    feature_other = trade(feature_mine, "col", 1)
    found_mine = jnp.concatenate([found, trade(found, "col", 2)], axis=0)
    found_other = trade(found_mine, "col", 1)
    (hidden,) = call(
        activate,
        [((nodes, width), BF16)],
        features,
        dense[:nodes],
        dense_got,
        inverse,
        w_self,
        w_neigh,
        bias,
    )
    results = [((nodes, width), BF16), ((width, width), F32), ((width, width), F32), ((1, width), F32)]
    grad_features, grad_self, grad_neigh, grad_bias = call(
        functools.partial(finish, 1.0 / math.sqrt(nodes * rows * cols)),
        results,
        found_mine,
        found_other,
        feature_mine,
        feature_other,
        own_columns,
        own_picks,
        w_self,
        w_neigh,
        scratch=[pltpu.VMEM((slots, width), BF16)] * 2
        + [pltpu.VMEM(*result) for result in results]
        + [pltpu.SemaphoreType.DMA((4,))],
        out_space=pl.ANY,
    )
    return (hidden, grad_features, grad_self, grad_neigh, grad_bias.reshape(width))


def tile_sum(values, take_index, put_index, usable, source, out_tiles, transpose, first_tile):
    slot_count, tile_width = (values.shape[0], values.shape[1])
    columns = source.shape[1]
    blocks = source.reshape(-1, tile_width, columns)
    group_size = math.gcd(slot_count, 16)
    pattern = "kji,kjf->kif" if transpose else "kij,kjf->kif"

    def advance(running, offset):
        tile_block = lax.dynamic_slice_in_dim(values, offset, group_size, 0)
        taken = lax.dynamic_slice_in_dim(take_index, offset, group_size, 0)
        placed = lax.dynamic_slice_in_dim(put_index, offset, group_size, 0) - first_tile
        allowed = lax.dynamic_slice_in_dim(usable, offset, group_size, 0)
        inside = allowed & (placed >= 0) & (placed < out_tiles)
        chosen = blocks[taken]
        product = jnp.einsum(pattern, tile_block, chosen, preferred_element_type=jnp.float32)
        product = product * inside.astype(jnp.float32)[:, None, None]
        where_to = jnp.where(inside, placed, 0)
        running = running.at[where_to].add(product)
        return (running, None)

    offsets = jnp.arange(0, slot_count, group_size, dtype=jnp.int32)
    running, _ = lax.scan(
        advance, jnp.zeros((out_tiles, tile_width, columns), jnp.float32), offsets
    )
    return running.reshape(out_tiles * tile_width, columns)


def dense_device(
    features,
    w_self,
    w_neigh,
    layer_bias,
    tile_vals,
    tile_dst,
    tile_src,
    tile_count,
    degree,
    target_ids,
    cotangent,
):
    row_count = lax.axis_size("row")
    col_count = lax.axis_size("col")
    node_rows = features.shape[0]
    tile_width = tile_vals.shape[-1]
    cell_tiles = tile_vals[0, 0]
    cell_dst = tile_dst[0, 0]
    cell_src = tile_src[0, 0]
    usable = jnp.arange(cell_tiles.shape[0], dtype=jnp.int32) < tile_count[0, 0]
    source = lax.all_gather(features, "row", axis=0, tiled=True)
    partial_value = tile_sum(
        cell_tiles,
        cell_src,
        cell_dst,
        usable,
        source,
        col_count * node_rows // tile_width,
        False,
        0,
    )
    agg_sum = lax.psum_scatter(partial_value, "col", scatter_dimension=0, tiled=True)
    inv_degree = 1.0 / degree.astype(jnp.float32)
    aggregate = (agg_sum * inv_degree[:, None]).astype(jnp.bfloat16)
    before = (
        jnp.dot(features, w_self, preferred_element_type=jnp.float32)
        + jnp.dot(aggregate, w_neigh, preferred_element_type=jnp.float32)
        + layer_bias
    )
    hidden = gelu_value(before).astype(jnp.bfloat16)
    first_node = (lax.axis_index("row") * col_count + lax.axis_index("col")) * node_rows
    node_ids = first_node + jnp.arange(node_rows, dtype=jnp.int32)
    target = jnp.any(node_ids[:, None] == target_ids[None, :], axis=1).astype(jnp.float32)
    slope_grad = (cotangent.astype(jnp.float32) * target[:, None] * gelu_slope(before)).astype(
        jnp.bfloat16
    )
    grad_scale = 1.0 / math.sqrt(node_rows * row_count * col_count)
    contract_rows = (((0,), (0,)), ((), ()))
    self_term = lax.dot_general(
        features, slope_grad, contract_rows, preferred_element_type=jnp.float32
    )
    neigh_term = lax.dot_general(
        aggregate, slope_grad, contract_rows, preferred_element_type=jnp.float32
    )
    bias_term = jnp.sum(slope_grad.astype(jnp.float32), axis=0)
    self_sum, neigh_sum, bias_sum = lax.psum((self_term, neigh_term, bias_term), ("row", "col"))
    contract_out = (((1,), (1,)), ((), ()))
    message = (
        lax.dot_general(slope_grad, w_neigh, contract_out, preferred_element_type=jnp.float32)
        * inv_degree[:, None]
    ).astype(jnp.bfloat16)
    message_slab = lax.all_gather(message, "col", axis=0, tiled=True)
    back_part = tile_sum(
        cell_tiles,
        cell_dst,
        cell_src,
        usable,
        message_slab,
        row_count * node_rows // tile_width,
        True,
        0,
    )
    neighbour_grad = lax.psum_scatter(
        back_part.astype(jnp.bfloat16).astype(jnp.float32).astype(jnp.bfloat16),
        "row",
        scatter_dimension=0,
        tiled=True,
    ).astype(jnp.float32)
    direct = lax.dot_general(slope_grad, w_self, contract_out, preferred_element_type=jnp.float32)
    grad_features = (direct + neighbour_grad).astype(jnp.bfloat16)
    return (
        hidden,
        grad_features,
        self_sum * grad_scale,
        neigh_sum * grad_scale,
        bias_sum * grad_scale,
    )


def solution(mesh):
    in_specs = (
        P(("groups", "row", "col"), None),
        P(),
        P(),
        P(),
        P(("groups", "row"), "col", None, None, None),
        P(("groups", "row"), "col", None),
        P(("groups", "row"), "col", None),
        P(("groups", "row"), "col"),
        P(("groups", "row", "col")),
        P("groups"),
        P(("groups", "row", "col"), None),
    )
    out_specs = (
        P(("groups", "row", "col"), None),
        P(("groups", "row", "col"), None),
        P("groups", None),
        P("groups", None),
        P("groups"),
    )
    four = mesh.shape["row"] == 4 and mesh.shape["col"] == 4

    def per_device(*args):
        tiles_are_owned_blocks = args[0].shape[0] == args[4].shape[-1] == 128
        return (compact_device if four and tiles_are_owned_blocks else dense_device)(*args)

    return jax.shard_map(
        per_device, mesh=mesh, in_specs=in_specs, out_specs=out_specs, check_vma=False
    )
```

```python
import functools
import itertools
import math

import jax
import jax.numpy as jnp
from jax import lax
from jax.experimental import pallas as pl
from jax.experimental.pallas import tpu as pltpu
from jax.sharding import PartitionSpec as P

F32 = jnp.float32
BF16 = jnp.bfloat16


def gelu_value(inputs):
    return 0.5 * inputs * (1.0 + jax.scipy.special.erf(inputs * 0.7071067811865476))


def gelu_slope(inputs):
    return (
        0.5 * (1.0 + jax.scipy.special.erf(inputs * 0.7071067811865476))
        + inputs * jnp.exp(-0.5 * inputs * inputs) * 0.3989422804014327
    )


def dot(left, right, dims=((1,), (0,))):
    return lax.dot_general(left, right, (dims, ((), ())), preferred_element_type=F32)


def trade(block, axis, step):
    return lax.ppermute(block, axis, [(i, i ^ step) for i in range(lax.axis_size(axis))])


def swap_quarters(line):
    first, second, third, last = jnp.split(line, 4, axis=1)
    return jnp.concatenate([first, third, second, last], axis=1)


def flip(line, parts, bit):
    cut = jnp.split(line, parts, axis=1)
    turned = [cut[i ^ 1] for i in range(parts)]
    return jnp.where(bit == 1, jnp.concatenate(turned, axis=1), line)


MERGE_COST = pl.CostEstimate(flops=2 * 10**9, bytes_accessed=0, transcendentals=0)
DENSE_COST = pl.CostEstimate(flops=3 * 10**9, bytes_accessed=0, transcendentals=0)


def call(kernel, outputs, *inputs, spaces=(), scratch=(), out_space=pltpu.VMEM, cost=None):
    inputs = [
        pltpu.with_memory_space_constraint(x, y) if y == pltpu.HBM else x
        for x, y in itertools.zip_longest(inputs, spaces)
    ]
    spaces = list(spaces) + [pltpu.VMEM] * (len(inputs) - len(spaces))
    return pl.pallas_call(
        kernel,
        out_shape=[jax.ShapeDtypeStruct(shape, dtype) for shape, dtype in outputs],
        in_specs=[pl.BlockSpec(memory_space=space) for space in spaces],
        out_specs=[pl.BlockSpec(memory_space=out_space) for _ in outputs],
        scratch_shapes=scratch,
        cost_estimate=cost,
        compiler_params=pltpu.CompilerParams(vmem_limit_bytes=32 * 2**20),
    )(*inputs)


def spread(block, axis, steps):
    return {step: trade(block, axis, step) for step in steps}


def swap_bits(index):
    return index // 2 + index % 2 * 2


def select(rows, cols, ids_in, src_in, dst_in, count_in, tiles_in, cotangent_in, degree_in, *refs):
    weights_in, refs = refs[:4], refs[4:]
    adjacency, column_picks, own_picks, known, near, far, inverse, *refs = refs
    weights, (picks, src, dst, count, tiles, cotangent, degree, ids, sems) = refs[:4], refs[4:]
    pairs = [(ids_in, ids), (cotangent_in, cotangent), (degree_in, degree), (tiles_in, tiles)]
    pairs += [(src_in, src), (dst_in, dst), (count_in, count)]
    pairs += list(zip(weights_in, weights))
    copies = [pltpu.make_async_copy(a, b, sems.at[i]) for i, (a, b) in enumerate(pairs)]
    for copy in copies:
        copy.start()
    row, col = lax.axis_index("row"), lax.axis_index("col")
    slots, (nodes, width) = ids.shape[1], cotangent.shape
    adjacency[...] = jnp.zeros(adjacency.shape, adjacency.dtype)
    copies[0].wait()
    line = flip(flip(swap_quarters(ids[...]), 2, col % 2), 4, col // 2)
    line = jnp.broadcast_to(line, (nodes, slots))
    stack = line.T
    lanes = lax.broadcasted_iota(jnp.int32, (slots, nodes), 1)
    for k in range(cols):
        base = (row * cols + (col ^ swap_bits(k))) * nodes
        picks[:, k * nodes : (k + 1) * nodes] = (stack == lanes + base).astype(BF16)
    for s in range(rows):
        base = ((row ^ s) * cols + col) * nodes
        column_picks[:, s * nodes : (s + 1) * nodes] = (stack == lanes + base).astype(BF16)
    base = (row * cols + col) * nodes
    across = lax.broadcasted_iota(jnp.int32, (nodes, slots), 0)
    own_picks[...] = (line == across + base).astype(BF16)
    for copy in copies[1:3]:
        copy.wait()
    own = picks[:, :nodes]
    known[:, :width] = dot(own, cotangent[...]).astype(BF16)
    counts = degree[...].astype(F32)
    inverse[...] = 1.0 / jnp.broadcast_to(counts, (nodes, nodes)).T
    counts = jnp.sum(own.astype(F32) * counts, axis=1, keepdims=True)
    known[:, width:] = jnp.broadcast_to(counts, (slots, 128)).astype(BF16)
    for copy in copies[3:7]:
        copy.wait()
    for k in range(tiles.shape[2]):

        @pl.when(k < count[0, 0])
        def _():
            down = pl.multiple_of(swap_bits(dst[0, 0, k] ^ col) * nodes, nodes)
            adjacency[src[0, 0, k] ^ row, pl.ds(down, nodes), :] = tiles[0, 0, k]

    for s in range(rows):
        block = dot(picks[...], adjacency[s]).astype(BF16)
        (far if s // 2 else near)[s % 2 * slots : (s % 2 + 1) * slots, :] = block
    for copy in copies[7:]:
        copy.wait()


def block_of(step, near, far, slots):
    return (far if step // 2 else near)[step % 2 * slots : (step % 2 + 1) * slots, :]


def dense_part(steps, adjacency, *refs):
    *features, kept, sent = refs
    total = sum(dot(adjacency[step], block[...]) for step, block in zip(steps, features))
    half = kept.shape[0]
    kept[...] = total[:half]
    sent[...] = total[half:].astype(BF16)


def combine(steps, column_picks, known, *refs):
    features, (near, far, sent, part, fixed) = refs[: len(steps)], refs[len(steps) :]
    nodes, width = features[0].shape
    half = part.shape[0]
    sums, picked = 0.0, 0.0
    for step, block in zip(steps, features):
        sums += dot(block_of(step, near, far, 2 * half), block[...])
        picked += dot(column_picks[:, step * nodes : (step + 1) * nodes], block[...])
    picked = picked.astype(BF16)
    part[...] = sums[:half]
    fixed[:, :width] = picked[:half]
    fixed[:, width:] = known[:half, :]
    sent[:, :width] = sums[half:].astype(BF16)
    sent[:, width : 2 * width] = picked[half:]
    sent[:, 2 * width :] = known[half:, :]


def relay(part, fixed, got, sent, part_out, fixed_out):
    share, width = part_out.shape
    sums = part[...] + got[:, :width].astype(F32)
    rest = fixed[...] + got[:, width:]
    part_out[...] = sums[:share]
    fixed_out[...] = rest[:share]
    sent[:, :width] = sums[share:].astype(BF16)
    sent[:, width:] = rest[share:]


def slopes(part, fixed, got, w_self, w_neigh, layer_bias, found, features):
    width = part.shape[1]
    total = part[...] + got[:, :width].astype(F32)
    rest = fixed[...] + got[:, width:]
    features[...] = rest[:, :width]
    cotangent = rest[:, width : 2 * width].astype(F32)
    degrees = rest[:, 2 * width :]
    degree = degrees[:, :1].astype(F32)
    inverse = jnp.where(degree > 0, 1.0 / jnp.maximum(degree, 1.0), 0.0)
    aggregate = (total * inverse).astype(BF16)
    before = dot(rest[:, :width], w_self[...]) + dot(aggregate, w_neigh[...]) + layer_bias[...]
    slope = (cotangent * gelu_slope(before)).astype(BF16)
    share, bands = part.shape[0], width // 128
    for b in range(bands):
        found[b * share : (b + 1) * share, :] = slope[:, b * 128 : (b + 1) * 128]
        down = (bands + b) * share
        found[down : down + share, :] = aggregate[:, b * 128 : (b + 1) * 128]
    line = degrees.astype(F32).T[:16, :]
    line = jnp.concatenate([line, jnp.zeros((16, 128 - share), F32)], axis=1)
    found[2 * bands * share :, :] = line.astype(BF16)


def merge(*refs):
    refs[-1][...] = sum(part[...] for part in refs[:-1])


def activate(features, total, got, inverse, w_self, w_neigh, layer_bias, hidden):
    total = total[...] + got[...].astype(F32)
    aggregate = (total * inverse[:, :1]).astype(BF16)
    before = dot(features[...], w_self[...]) + dot(aggregate, w_neigh[...]) + layer_bias[...]
    hidden[...] = gelu_value(before).astype(BF16)


def finish(scale, *refs):
    found, features, refs = refs[:2], refs[2:4], refs[4:]
    own_columns, own_picks, w_self, w_neigh, *refs = refs
    outs, (slope, aggregate, *results, sems) = refs[:4], refs[4:]
    grad_features, grad_self, grad_neigh, grad_bias = results
    slots, width = slope.shape
    half, bands = slots // 2, width // 128
    share = half // 2
    size = found[0].shape[0] // 2
    front, back = ((0,), (0,)), ((1,), (1,))
    degrees = []
    for q in range(4):
        part, base, here = found[q // 2], q % 2 * size, slice(q * share, (q + 1) * share)
        for b in range(bands):
            lanes = slice(b * 128, (b + 1) * 128)
            slope[here, lanes] = part[base + b * share : base + (b + 1) * share, :]
            down = base + (bands + b) * share
            aggregate[here, lanes] = part[down : down + share, :]
        degrees.append(part[base + size - 16 : base + size, :].astype(F32)[:1, :share])
    copies = [pltpu.make_async_copy(a, b, sems.at[i]) for i, (a, b) in enumerate(zip(results, outs))]
    grad_self[...] = scale * (
        dot(features[0][...], slope[:half, :], front)
        + dot(features[1][...], slope[half:, :], front)
    )
    copies[1].start()
    grad_neigh[...] = dot(aggregate[...], slope[...], front) * scale
    copies[2].start()
    grad_bias[...] = jnp.sum(slope[...].astype(F32), axis=0, keepdims=True) * scale
    copies[3].start()
    degree = jnp.broadcast_to(jnp.concatenate(degrees, axis=1), (128, slots)).T[:, :1]
    message = (dot(slope[...], w_neigh[...], back) / degree).astype(BF16)
    own_slope = dot(own_picks[...], slope[...]).astype(BF16)
    total = dot(own_slope, w_self[...], back) + dot(own_columns[...], message, front)
    grad_features[...] = total.astype(BF16)
    copies[0].start()
    for copy in copies:
        copy.wait()


def compact_device(
    features,
    w_self,
    w_neigh,
    layer_bias,
    tile_vals,
    tile_dst,
    tile_src,
    tile_count,
    degree,
    target_ids,
    cotangent,
):
    rows = lax.axis_size("row")
    cols = lax.axis_size("col")
    nodes, width = features.shape
    slots = target_ids.shape[0]
    share = slots // cols
    half = slots // 2

    order = (3, 1, 2)
    feature_parts = spread(features, "row", order)

    bias = layer_bias.reshape(1, width)
    adjacency, column_picks, own_picks, known, near, far, inverse, *resident = call(
        functools.partial(select, rows, cols),
        [
            ((rows, cols * nodes, nodes), BF16),
            ((slots, rows * nodes), BF16),
            ((nodes, slots), BF16),
            ((slots, width + 128), BF16),
        ]
        + [((rows // 2 * slots, nodes), BF16)] * 2
        + [((nodes, nodes), F32)]
        + [((width, width), BF16)] * 2
        + [((1, width), F32), ((nodes, width), BF16)],
        target_ids.reshape(1, slots),
        tile_src,
        tile_dst,
        tile_count,
        tile_vals,
        cotangent,
        degree.reshape(1, nodes),
        w_self,
        w_neigh,
        bias,
        features,
        spaces=[pltpu.HBM] * 3 + [pl.ANY] + [pltpu.HBM] * 7,
        scratch=[pltpu.VMEM((slots, cols * nodes), BF16)]
        + [pltpu.SMEM(x.shape, x.dtype) for x in (tile_src, tile_dst, tile_count)]
        + [pltpu.VMEM(x.shape, x.dtype) for x in (tile_vals, cotangent)]
        + [pltpu.VMEM((1, nodes), jnp.int32), pltpu.VMEM((1, slots), jnp.int32)]
        + [pltpu.SemaphoreType.DMA((11,))],
    )
    w_self, w_neigh, bias, features = resident
    feature_parts[0] = features
    sent, part, fixed = call(
        functools.partial(combine, order + (0,)),
        [((half, 3 * width + 128), BF16), ((half, width), F32), ((half, 2 * width + 128), BF16)],
        column_picks,
        known,
        *[feature_parts[step] for step in order + (0,)],
        near,
        far,
    )
    got = trade(sent, "col", 1)
    sent, part, fixed = call(
        relay,
        [((share, 3 * width + 128), BF16), ((share, width), F32), ((share, 2 * width + 128), BF16)],
        part,
        fixed,
        got,
    )
    got = trade(sent, "col", 2)
    found, feature_slots = call(
        slopes,
        [((2 * (width // 128) * share + 16, 128), BF16), ((share, width), BF16)],
        part,
        fixed,
        got,
        w_self,
        w_neigh,
        bias,
    )
    columns = near + trade(far, "row", 2)
    found, columns = lax.optimization_barrier((found, columns))
    dense, dense_sent = call(
        functools.partial(dense_part, order + (0,)),
        [((2 * nodes, width), F32), ((2 * nodes, width), BF16)],
        adjacency,
        *[feature_parts[step] for step in order + (0,)],
        cost=DENSE_COST,
    )
    dense = dense + trade(dense_sent, "col", 1).astype(F32)
    parts = spread(found, "row", order)
    (found,) = call(merge, [(found.shape, BF16)], parts.pop(order[0]), found, cost=MERGE_COST)
    found, feature_slots = lax.optimization_barrier((found, feature_slots))
    found, dense = lax.optimization_barrier((found, dense))
    (found,) = call(merge, [(found.shape, BF16)], *parts.values(), found, cost=MERGE_COST)
    own_columns = columns[:slots] + trade(columns[slots:], "row", 1)
    dense_got = trade(dense[nodes:].astype(BF16), "col", 2)
    feature_mine = jnp.concatenate([feature_slots, trade(feature_slots, "col", 2)], axis=0)
    feature_other = trade(feature_mine, "col", 1)
    found_mine = jnp.concatenate([found, trade(found, "col", 2)], axis=0)
    found_other = trade(found_mine, "col", 1)
    (hidden,) = call(
        activate,
        [((nodes, width), BF16)],
        features,
        dense[:nodes],
        dense_got,
        inverse,
        w_self,
        w_neigh,
        bias,
    )
    results = [((nodes, width), BF16), ((width, width), F32), ((width, width), F32), ((1, width), F32)]
    grad_features, grad_self, grad_neigh, grad_bias = call(
        functools.partial(finish, 1.0 / math.sqrt(nodes * rows * cols)),
        results,
        found_mine,
        found_other,
        feature_mine,
        feature_other,
        own_columns,
        own_picks,
        w_self,
        w_neigh,
        scratch=[pltpu.VMEM((slots, width), BF16)] * 2
        + [pltpu.VMEM(*result) for result in results]
        + [pltpu.SemaphoreType.DMA((4,))],
        out_space=pl.ANY,
    )
    return (hidden, grad_features, grad_self, grad_neigh, grad_bias.reshape(width))


def tile_sum(values, take_index, put_index, usable, source, out_tiles, transpose, first_tile):
    slot_count, tile_width = (values.shape[0], values.shape[1])
    columns = source.shape[1]
    blocks = source.reshape(-1, tile_width, columns)
    group_size = math.gcd(slot_count, 16)
    pattern = "kji,kjf->kif" if transpose else "kij,kjf->kif"

    def advance(running, offset):
        tile_block = lax.dynamic_slice_in_dim(values, offset, group_size, 0)
        taken = lax.dynamic_slice_in_dim(take_index, offset, group_size, 0)
        placed = lax.dynamic_slice_in_dim(put_index, offset, group_size, 0) - first_tile
        allowed = lax.dynamic_slice_in_dim(usable, offset, group_size, 0)
        inside = allowed & (placed >= 0) & (placed < out_tiles)
        chosen = blocks[taken]
        product = jnp.einsum(pattern, tile_block, chosen, preferred_element_type=jnp.float32)
        product = product * inside.astype(jnp.float32)[:, None, None]
        where_to = jnp.where(inside, placed, 0)
        running = running.at[where_to].add(product)
        return (running, None)

    offsets = jnp.arange(0, slot_count, group_size, dtype=jnp.int32)
    running, _ = lax.scan(
        advance, jnp.zeros((out_tiles, tile_width, columns), jnp.float32), offsets
    )
    return running.reshape(out_tiles * tile_width, columns)


def dense_device(
    features,
    w_self,
    w_neigh,
    layer_bias,
    tile_vals,
    tile_dst,
    tile_src,
    tile_count,
    degree,
    target_ids,
    cotangent,
):
    row_count = lax.axis_size("row")
    col_count = lax.axis_size("col")
    node_rows = features.shape[0]
    tile_width = tile_vals.shape[-1]
    cell_tiles = tile_vals[0, 0]
    cell_dst = tile_dst[0, 0]
    cell_src = tile_src[0, 0]
    usable = jnp.arange(cell_tiles.shape[0], dtype=jnp.int32) < tile_count[0, 0]
    source = lax.all_gather(features, "row", axis=0, tiled=True)
    partial_value = tile_sum(
        cell_tiles,
        cell_src,
        cell_dst,
        usable,
        source,
        col_count * node_rows // tile_width,
        False,
        0,
    )
    agg_sum = lax.psum_scatter(partial_value, "col", scatter_dimension=0, tiled=True)
    inv_degree = 1.0 / degree.astype(jnp.float32)
    aggregate = (agg_sum * inv_degree[:, None]).astype(jnp.bfloat16)
    before = (
        jnp.dot(features, w_self, preferred_element_type=jnp.float32)
        + jnp.dot(aggregate, w_neigh, preferred_element_type=jnp.float32)
        + layer_bias
    )
    hidden = gelu_value(before).astype(jnp.bfloat16)
    first_node = (lax.axis_index("row") * col_count + lax.axis_index("col")) * node_rows
    node_ids = first_node + jnp.arange(node_rows, dtype=jnp.int32)
    target = jnp.any(node_ids[:, None] == target_ids[None, :], axis=1).astype(jnp.float32)
    slope_grad = (cotangent.astype(jnp.float32) * target[:, None] * gelu_slope(before)).astype(
        jnp.bfloat16
    )
    grad_scale = 1.0 / math.sqrt(node_rows * row_count * col_count)
    contract_rows = (((0,), (0,)), ((), ()))
    self_term = lax.dot_general(
        features, slope_grad, contract_rows, preferred_element_type=jnp.float32
    )
    neigh_term = lax.dot_general(
        aggregate, slope_grad, contract_rows, preferred_element_type=jnp.float32
    )
    bias_term = jnp.sum(slope_grad.astype(jnp.float32), axis=0)
    self_sum, neigh_sum, bias_sum = lax.psum((self_term, neigh_term, bias_term), ("row", "col"))
    contract_out = (((1,), (1,)), ((), ()))
    message = (
        lax.dot_general(slope_grad, w_neigh, contract_out, preferred_element_type=jnp.float32)
        * inv_degree[:, None]
    ).astype(jnp.bfloat16)
    message_slab = lax.all_gather(message, "col", axis=0, tiled=True)
    back_part = tile_sum(
        cell_tiles,
        cell_dst,
        cell_src,
        usable,
        message_slab,
        row_count * node_rows // tile_width,
        True,
        0,
    )
    neighbour_grad = lax.psum_scatter(
        back_part.astype(jnp.bfloat16).astype(jnp.float32).astype(jnp.bfloat16),
        "row",
        scatter_dimension=0,
        tiled=True,
    ).astype(jnp.float32)
    direct = lax.dot_general(slope_grad, w_self, contract_out, preferred_element_type=jnp.float32)
    grad_features = (direct + neighbour_grad).astype(jnp.bfloat16)
    return (
        hidden,
        grad_features,
        self_sum * grad_scale,
        neigh_sum * grad_scale,
        bias_sum * grad_scale,
    )


def solution(mesh):
    in_specs = (
        P(("groups", "row", "col"), None),
        P(),
        P(),
        P(),
        P(("groups", "row"), "col", None, None, None),
        P(("groups", "row"), "col", None),
        P(("groups", "row"), "col", None),
        P(("groups", "row"), "col"),
        P(("groups", "row", "col")),
        P("groups"),
        P(("groups", "row", "col"), None),
    )
    out_specs = (
        P(("groups", "row", "col"), None),
        P(("groups", "row", "col"), None),
        P("groups", None),
        P("groups", None),
        P("groups"),
    )
    four = mesh.shape["row"] == 4 and mesh.shape["col"] == 4

    def per_device(*args):
        tiles_are_owned_blocks = args[0].shape[0] == args[4].shape[-1] == 128
        return (compact_device if four and tiles_are_owned_blocks else dense_device)(*args)

    return jax.shard_map(
        per_device, mesh=mesh, in_specs=in_specs, out_specs=out_specs, check_vma=False
    )
```
